512 devices in a mesh: seq: 256 (over x, z, y_lo, core), rep: 2 (over y_hi).
Axes of the slice: x: 4, y: 4 (y_hi: 2, y_lo: 2; y = y_hi * 2 + y_lo), z: 16, core: 2. Of those that a mesh axis runs over, the one named last changes fastest.
Arguments:
- acts: bfloat16 [131072, 6144], P(('seq', 'rep')), may hold values from -24 to 24
- grad_logits: bfloat16 [131072, 128], P(('seq', 'rep')), may hold values from -0.017944336 to 0.017944336
- master: float32 [6144, 128], P('seq'), may hold values from -0.078125 to 0.078125
- moment_one: float32 [6144, 128], P('seq'), may hold values from -3 to 3
- moment_two: float32 [6144, 128], P('seq'), may hold values from 0.05 to 2
- step_count: int32 [1], replicated, may hold values from 1 to 40
Outputs:
- master_new: float32 [6144, 128], P('seq')
- moment_one_new: float32 [6144, 128], P('seq')
- moment_two_new: float32 [6144, 128], P('seq')
- logits_new: bfloat16 [131072, 128], P(('seq', 'rep'))
The draws below stay inside these ranges and needn't reach their ends.
All inputs are finite; a program needn't handle non-finite values.
Results may differ from the reference program's by a relative error of at most 0.0024.
The reference program's roundings to bfloat16 on the way count: a program that leaves them out, or rounds other values in their place, can miss the bound.
Values may be sent and summed in bfloat16 or wider, within the bound.
A program may use at most 64 MiB of HBM per device.

```python
import math
import jax
import jax.numpy as jnp
from jax import lax

D = 6144
E = 128
TOK_DEV = 256
TOKENS = 131072
N_SEQ = 256
N_REP = 2


def raised(result, stream_key, source, target, blocks, factor):
    owner, partner = [(jnp.arange(result.shape[position]) // (result.shape[position] // blocks)).reshape([-1 if axis == position else 1 for axis in range(result.ndim)]) for position in (source, target)]
    chosen = jax.random.permutation(stream_key, blocks)[partner]
    strong = (owner == chosen) | (owner == (partner + blocks // 2) % blocks)
    return jnp.where(strong, factor * result, result)


def levels(key, dims, pieces, least, top_value):
    def one(position, blocks):
        heights = jax.random.uniform(jax.random.fold_in(jax.random.fold_in(key, 6), position), (blocks,), jnp.float32, least / len(pieces), top_value / len(pieces))
        return jnp.repeat(jnp.exp(heights), dims[position] // blocks).reshape((-1,) + (1,) * (len(dims) - position - 1))

    level = one(*pieces[0])
    for cut in pieces[1:]:
        level = level * one(*cut)
    return level


def gaussian(rng, shape, deviation, most, pieces=(), held_as=jnp.bfloat16):
    factor_of = levels(rng, shape, pieces, -0.22, 0.18) if pieces else 1.0
    entries = jax.random.normal(rng, shape, jnp.float32) * deviation * factor_of
    return jnp.minimum(jnp.maximum(entries, -most), most).astype(held_as)


def gaussian_with(own_key, shape, width, reach, pieces, heavy, held_as=jnp.bfloat16):
    drawn = width * jax.random.normal(own_key, shape, jnp.float32)
    if pieces:
        drawn = drawn * levels(own_key, shape, pieces, -0.22, 0.18)
    return jnp.clip(raised(drawn, jax.random.fold_in(own_key, 3), *heavy), -reach, reach).astype(held_as)


def setup_inputs(seed: int = 0) -> dict:
    key_of = jax.random.split(jax.random.key(seed), 7)
    return {
        "acts": gaussian_with(key_of[0], (TOKENS, D), 1.0, 24.0, ((0, 512),), (0, 1, 512, 6.0)),
        "grad_logits": gaussian(key_of[1], (TOKENS, E), 0.003, 0.017944336, ((0, 512),)),
        "master": gaussian(key_of[2], (D, E), D ** -0.5, 0.078125, ((0, 256),), jnp.float32),
        "moment_one": gaussian(key_of[3], (D, E), 0.5, 3.0, ((0, 256),), jnp.float32),
        "moment_two": jnp.clip(jnp.exp(math.log(2.0) - 3.6888794 * jax.random.uniform(key_of[4], (D, E), jnp.float32) ** levels(key_of[4], (D, E), ((0, 256),), -0.2, 0.2)), 0.05, 2.0),
        "step_count": jax.random.randint(key_of[5], (1,), 1, 41).astype(jnp.int32),
    }


def reference(acts, grad_logits, master, moment_one, moment_two, step_count):
    blocks = N_SEQ * N_REP
    act_blocks = acts.reshape(blocks, TOK_DEV, D)
    grad_blocks = grad_logits.reshape(blocks, TOK_DEV, E)

    def accumulate(total, pair):
        piece = lax.dot_general(pair[0], pair[1], (((0,), (0,)), ((), ())), preferred_element_type=jnp.float32)
        rounded = lax.optimization_barrier(piece.astype(jnp.bfloat16))
        return (total + rounded.astype(jnp.float32), None)
    grad, _ = lax.scan(accumulate, jnp.zeros((D, E), jnp.float32), (act_blocks, grad_blocks))
    count = step_count[0].astype(jnp.float32)
    beta_one = 0.9
    beta_two = 0.95
    first = beta_one * moment_one + (1.0 - beta_one) * grad
    second = beta_two * moment_two + (1.0 - beta_two) * grad * grad
    first_hat = first / (1.0 - jnp.power(beta_one, count))
    second_hat = second / (1.0 - jnp.power(beta_two, count))
    updated = master - 0.01 * (first_hat / (jnp.sqrt(second_hat) + 1e-08) + 0.1 * master)
    weight_new = updated.astype(jnp.bfloat16)
    logits = jnp.dot(acts, weight_new, preferred_element_type=jnp.float32).astype(jnp.bfloat16)
    return (updated, first, second, logits)
```

```python
import math

import jax
import jax.numpy as jnp
from jax import lax
from jax.experimental import pallas as pl
from jax.experimental.pallas import tpu as pltpu
from jax.sharding import PartitionSpec as P

D = 6144
E = 128
TOK = 256
OWN = 24
UNIT = 48
BLK = 384
F32 = jnp.float32
BF16 = jnp.bfloat16
PAIRS = ((2, 0), (2, 1), (1, 0), (3, 0), (1, 1), (3, 1), (0, 1))
NEAR = ((0, 1), (1, 0), (3, 0), (1, 1), (3, 1), (2, 0), (2, 1))


def adam(grad, master, one, two, count):
    ones = jnp.ones((1, E), F32)
    first = 0.9 * one + (1.0 - 0.9) * grad
    second = 0.95 * two + (1.0 - 0.95) * grad * grad
    first_hat = first / (1.0 - jnp.exp(count * math.log(0.9) * ones))
    second_hat = second / (1.0 - jnp.exp(count * math.log(0.95) * ones))
    updated = master - 0.01 * (first_hat / (jnp.sqrt(second_hat) + 1e-08) + 0.1 * master)
    return updated, first, second


def kernel(
    step_ref, acts_hbm, glog_ref, master_ref, one_ref, two_ref,
    master_out, one_out, two_out, logits_out,
    acts, part, recv_a, acc, recv_b, unit, recv_c, own48, state, state48, grad_own, wnew,
    load_sem, st_sem, sa, ra, sb, rb, sc, rc, sd, rd, sz, rz, s1, r1, s2, r2, s3, r3,
):
    seq = lax.axis_index("seq")
    rep = lax.axis_index("rep")
    core = lax.rem(seq, 2)
    y = rep * 2 + lax.rem(seq // 2, 2)
    z = lax.rem(seq // 4, 16)
    x = seq // 64
    main = (x, y)
    cross = (y, x)

    def dev(px, py, pz, pc):
        return {"seq": ((px * 16 + pz) * 2 + lax.rem(py, 2)) * 2 + pc, "rep": py // 2}

    def at(h, dmain, dcross, dcore):
        dx, dy = (dmain, dcross) if h == 0 else (dcross, dmain)
        return dev(lax.rem(x + dx, 4), lax.rem(y + dy, 4), z, lax.rem(core + dcore, 2))

    def along_z(dz):
        return dev(x, y, lax.rem(z + dz, 16), core)

    barrier = pltpu.get_barrier_semaphore()
    loads = []
    for k in range(4):
        cols = pl.ds(k * 1536, 1536)
        load = pltpu.make_async_copy(acts_hbm.at[:, cols], acts.at[:, cols], load_sem.at[k])
        load.start()
        loads.append(load)
    for h in range(2):
        for d, e in PAIRS:
            if h == 1 and d == 0:
                continue
            pl.semaphore_signal(barrier, inc=1, device_id=at(h, d, 0, e), device_id_type=pl.DeviceIdType.MESH)
    for dz in range(1, 16):
        pl.semaphore_signal(barrier, inc=1, device_id=along_z(dz), device_id_type=pl.DeviceIdType.MESH)

    state[0] = master_ref[...]
    state[1] = one_ref[...]
    state[2] = two_ref[...]
    half = pl.ds(pl.multiple_of(core * OWN, 8), OWN)
    state48[:, half, :] = state[...]

    glog = glog_ref[...]
    for k in range(4):
        loads[k].wait()
        for zg in range(4):
            cols = pl.ds(k * 1536 + zg * BLK, BLK)
            product = lax.dot_general(
                acts[:, cols], glog, (((0,), (0,)), ((), ())), preferred_element_type=F32
            ).astype(BF16)
            for zr in range(4):
                for ylo in range(2):
                    piece = product[(zr * 2 + ylo) * UNIT:(zr * 2 + ylo + 1) * UNIT]
                    py = (zr // 2) * 2 + ylo
                    pc = zr % 2
                    if zg < 2:
                        part[0, k * 2 + pc, py * 96 + zg * UNIT:py * 96 + zg * UNIT + UNIT] = piece
                    else:
                        lo = k * 96 + (zg - 2) * UNIT
                        part[1, py * 2 + pc, lo:lo + UNIT] = piece

    pl.semaphore_wait(barrier, 28)

    def remote(src, dst, send, recv, device):
        return pltpu.make_async_remote_copy(
            src_ref=src, dst_ref=dst, send_sem=send, recv_sem=recv,
            device_id=device, device_id_type=pl.DeviceIdType.MESH,
        )

    sent = []
    copy_a = {}
    for d, e in PAIRS:
        for h in range(2):
            place = lax.rem(main[h] + d, 4) * 2 + lax.rem(core + e, 2)
            copy = remote(
                part.at[h, place], recv_a.at[h, d * 2 + e], sa.at[h, d * 2 + e], ra.at[h, d * 2 + e],
                at(h, d, 0, e),
            )
            copy.start()
            copy_a[h, d, e] = copy
            sent.append(copy)
    state_copy = remote(state, state48.at[:, half, :], st_sem.at[0], st_sem.at[1], at(0, 0, 0, 1))
    state_copy.start()
    sent.append(state_copy)

    copy_b = {}
    for h in range(2):
        mine = main[h] * 2 + core
        for d, e in NEAR:
            copy_a[h, d, e].wait_recv()
        for d in (2, 1, 3, 0):
            to = lax.rem(cross[h] + d, 4)
            rows = pl.ds(pl.multiple_of(to * 96, 16), 96)
            total = part[h, mine, rows].astype(F32)
            for p, e in NEAR:
                total = total + recv_a[h, p * 2 + e, rows].astype(F32)
            acc[h, d] = total
            if d:
                copy = remote(acc.at[h, d], recv_b.at[h, d], sb.at[h, d], rb.at[h, d], at(h, 0, d, 0))
                copy.start()
                copy_b[h, d] = copy
                sent.append(copy)

    mod = rep * 2 + core
    primary = lax.rem(z, 4) == mod
    copy_c = []
    for h in range(2):
        for d in (1, 3, 2):
            copy_b[h, d].wait_recv()
        total = ((acc[h, 0] + recv_b[h, 1]) + recv_b[h, 3]) + recv_b[h, 2]
        for k in range(2):
            zg = h * 2 + k
            unit[zg] = total[k * UNIT:(k + 1) * UNIT]
            to = zg * 4 + mod
            dz = lax.rem(to + 16 - z, 16)
            copy = remote(unit.at[zg], recv_c.at[dz], sc.at[zg], rc.at[dz], dev(x, y, to, core))
            copy_c.append((copy, dz))

            @pl.when(dz != 0)
            def _():
                copy.start()

            @pl.when(dz == 0)
            def _():
                own48[...] = unit[zg]

    count = step_ref[0].astype(F32)
    state_copy.wait_recv()
    other = pl.ds(pl.multiple_of((1 - core) * OWN, 8), OWN)

    def place(h, k):
        which = x * (1 - h) + y * h
        inner = y * (1 - h) + x * h
        return wnew.at[h, which * 2 + core, pl.ds(pl.multiple_of(inner * 96 + k * UNIT, 16), UNIT)]

    zg_me = z // 4
    spot = place(zg_me // 2, lax.rem(zg_me, 2))
    copy_z = [
        remote(spot, spot, sz.at[dz], rz.at[zg_me], along_z(dz)) for dz in range(1, 16)
    ]
    copy_d = [
        remote(own48.at[half], grad_own, sd.at[0], rd.at[0], at(1, 2, 0, 0)),
        remote(own48.at[other], grad_own, sd.at[1], rd.at[0], at(1, 0, 0, 1)),
        remote(own48.at[other], grad_own, sd.at[2], rd.at[0], at(1, 2, 0, 1)),
    ]

    @pl.when(primary)
    def _():
        for dz in range(1, 16):
            remote(recv_c.at[dz], recv_c.at[dz], sc.at[0], rc.at[dz], along_z(dz)).wait_recv()
        total = own48[...]
        for dz in range(1, 16):
            total = total + recv_c[dz]
        updated, _, _ = adam(total, state48[0], state48[1], state48[2], count)
        spot[...] = updated.astype(BF16)
        for dz in (8, 7, 9, 6, 10, 5, 11, 4, 12, 3, 13, 2, 14, 1, 15):
            copy_z[dz - 1].start()
        own48[...] = total
        for copy in copy_d:
            copy.start()
        grad_own[...] = own48[half]

    copy_1 = {}
    for h in range(2):
        for k in range(2):
            zg = h * 2 + k

            @pl.when(z != zg * 4 + mod)
            def _():
                remote(place(h, k), place(h, k), sz.at[0], rz.at[zg], along_z(1)).wait_recv()
        rows = wnew.at[h, main[h] * 2 + core, pl.ds(pl.multiple_of(cross[h] * 96, 16), 96)]
        for d in (2, 1, 3):
            copy = remote(rows, rows, s1.at[h, d], r1.at[h, d], at(h, 0, d, 0))
            copy.start()
            copy_1[h, d] = copy
            sent.append(copy)

    copy_2 = {}
    copy_3 = {}

    def forward(h, d):
        lane = wnew.at[h, lax.rem(main[h] + d, 4) * 2 + core]
        copy = remote(lane, lane, s3.at[h, d], r3.at[h, d], at(h, 0, 0, 1))
        copy.start()
        copy_3[h, d] = copy
        sent.append(copy)

    for h in range(2):
        for d in (1, 3, 2):
            copy_1[h, d].wait_recv()
        block = wnew.at[h, main[h] * 2 + core]
        for d in (2, 1, 3):
            copy = remote(block, block, s2.at[h, d], r2.at[h, d], at(h, d, 0, 0))
            copy.start()
            copy_2[h, d] = copy
            sent.append(copy)
        forward(h, 0)

    @pl.when(jnp.logical_not(primary))
    def _():
        remote(grad_own, grad_own, sd.at[0], rd.at[0], at(1, 2, 0, 0)).wait_recv()

    updated, first, second = adam(grad_own[...], state[0], state[1], state[2], count)
    master_out[...] = updated
    one_out[...] = first
    two_out[...] = second

    for d in (1, 3, 2):
        for h in range(2):
            copy_2[h, d].wait_recv()
            forward(h, 4 - d)
    for d in (0, 1, 3, 2):
        for h in range(2):
            copy_3[h, d].wait_recv()

    total = jnp.zeros((TOK, E), F32)
    for k in range(4):
        for zg in range(4):
            pieces = []
            for zr in range(4):
                for ylo in range(2):
                    py = (zr // 2) * 2 + ylo
                    pc = zr % 2
                    if zg < 2:
                        lo = py * 96 + zg * UNIT
                        pieces.append(wnew[0, k * 2 + pc, lo:lo + UNIT])
                    else:
                        lo = k * 96 + (zg - 2) * UNIT
                        pieces.append(wnew[1, py * 2 + pc, lo:lo + UNIT])
            cols = pl.ds(k * 1536 + zg * BLK, BLK)
            total = total + jnp.dot(
                acts[:, cols], jnp.concatenate(pieces, axis=0), preferred_element_type=F32
            )
    logits_out[...] = total.astype(BF16)

    for copy in sent:
        copy.wait_send()
    for copy, dz in copy_c:
        @pl.when(dz != 0)
        def _():
            copy.wait_send()

    @pl.when(primary)
    def _():
        for copy in copy_z:
            copy.wait_send()
        for copy in copy_d:
            copy.wait_send()


def per_device(acts, grad_logits, master, moment_one, moment_two, step_count):
    vmem = pl.BlockSpec(memory_space=pltpu.VMEM)
    dma = pltpu.SemaphoreType.DMA
    own = jax.ShapeDtypeStruct((OWN, E), F32)
    return pl.pallas_call(
        kernel,
        out_shape=(own, own, own, jax.ShapeDtypeStruct((TOK, E), BF16)),
        in_specs=[
            pl.BlockSpec(memory_space=pltpu.SMEM), pl.BlockSpec(memory_space=pl.ANY), vmem, vmem, vmem, vmem,
        ],
        out_specs=(vmem, vmem, vmem, vmem),
        scratch_shapes=[
            pltpu.VMEM((TOK, D), BF16),
            pltpu.VMEM((2, 8, BLK, E), BF16),
            pltpu.VMEM((2, 8, BLK, E), BF16),
            pltpu.VMEM((2, 4, 96, E), F32),
            pltpu.VMEM((2, 4, 96, E), F32),
            pltpu.VMEM((4, UNIT, E), F32),
            pltpu.VMEM((16, UNIT, E), F32),
            pltpu.VMEM((UNIT, E), F32),
            pltpu.VMEM((3, OWN, E), F32),
            pltpu.VMEM((3, UNIT, E), F32),
            pltpu.VMEM((OWN, E), F32),
            pltpu.VMEM((2, 8, BLK, E), BF16),
            dma((4,)), dma((2,)),
            dma((2, 8)), dma((2, 8)),
            dma((2, 4)), dma((2, 4)),
            dma((4,)), dma((16,)),
            dma((3,)), dma((1,)),
            dma((16,)), dma((4,)),
            dma((2, 4)), dma((2, 4)),
            dma((2, 4)), dma((2, 4)),
            dma((2, 4)), dma((2, 4)),
        ],
        compiler_params=pltpu.CompilerParams(
            collective_id=0, has_side_effects=True, vmem_limit_bytes=32 * 1024 * 1024
        ),
        cost_estimate=pl.CostEstimate(flops=4 * TOK * D * E, bytes_accessed=3 * 1024 * 1024, transcendentals=0),
    )(step_count, acts, grad_logits, master, moment_one, moment_two)


def solution(mesh):
    in_specs = (
        P(("seq", "rep"), None),
        P(("seq", "rep"), None),
        P("seq", None),
        P("seq", None),
        P("seq", None),
        P(),
    )
    out_specs = (P("seq", None), P("seq", None), P("seq", None), P(("seq", "rep"), None))
    return jax.shard_map(
        per_device, mesh=mesh, in_specs=in_specs, out_specs=out_specs, check_vma=False
    )
```

```python
import math

import jax
import jax.numpy as jnp
from jax import lax
from jax.experimental import pallas as pl
from jax.experimental.pallas import tpu as pltpu
from jax.sharding import PartitionSpec as P

D = 6144
E = 128
TOK = 256
OWN = 24
UNIT = 48
BLK = 384
F32 = jnp.float32
BF16 = jnp.bfloat16
PAIRS = ((2, 0), (2, 1), (1, 0), (3, 0), (1, 1), (3, 1), (0, 1))
STEPS = (2, 1, 3, 0)
ORDER = (0, 1, 2, 3, 4, 5, 6, 7, 15, 14, 13, 8, 12, 9, 10, 11)
NEAR = ((0, 1), (1, 0), (3, 0), (1, 1), (3, 1), (2, 0), (2, 1))


def adam(grad, master, one, two, count):
    ones = jnp.ones((1, E), F32)
    first = 0.9 * one + (1.0 - 0.9) * grad
    second = 0.95 * two + (1.0 - 0.95) * grad * grad
    first_hat = first / (1.0 - jnp.exp(count * math.log(0.9) * ones))
    second_hat = second / (1.0 - jnp.exp(count * math.log(0.95) * ones))
    updated = master - 0.01 * (first_hat / (jnp.sqrt(second_hat) + 1e-08) + 0.1 * master)
    return updated, first, second


def kernel(
    step_hbm, acts_hbm, glog_hbm, master_hbm, one_hbm, two_hbm,
    grad_out, logits_out,
    step_ref, acts, glog_ref, part, recv_a, acc, recv_b, unit, recv_c, own48, state, state48, grad_own, wnew,
    load_sem, st_sem, ready, sa, ra, sb, rb, sc, rc, sd, rd, sz, rz, s1, r1, s2, r2, s3, r3,
):
    seq = lax.axis_index("seq")
    rep = lax.axis_index("rep")
    core = lax.rem(seq, 2)
    y = rep * 2 + lax.rem(seq // 2, 2)
    z = lax.rem(seq // 4, 16)
    x = seq // 64
    main = (x, y)
    cross = (y, x)

    def dev(px, py, pz, pc):
        return {"seq": ((px * 16 + pz) * 2 + lax.rem(py, 2)) * 2 + pc, "rep": py // 2}

    def at(h, dmain, dcross, dcore):
        dx, dy = (dmain, dcross) if h == 0 else (dcross, dmain)
        return dev(lax.rem(x + dx, 4), lax.rem(y + dy, 4), z, lax.rem(core + dcore, 2))

    def along_z(dz):
        return dev(x, y, lax.rem(z + dz, 16), core)

    def load(src, dst, number):
        copy = pltpu.make_async_copy(src, dst, load_sem.at[number])
        copy.start()
        return copy

    barrier = pltpu.get_barrier_semaphore()
    glog_load = load(glog_hbm, glog_ref, 8)
    loads_two = []
    for k in range(4):
        cols = pl.ds(k * 1536 + 768, 768)
        loads_two.append(load(acts_hbm.at[:, cols], acts.at[:, cols], 4 + k))
    loads_one = {}
    for d in STEPS:
        cols = pl.ds(pl.multiple_of(lax.rem(x + d, 4) * 1536, 128), 768)
        loads_one[d] = load(acts_hbm.at[:, cols], acts.at[:, cols], d)
    loads_state = [load(ref, state.at[k], 9 + k) for k, ref in enumerate((master_hbm, one_hbm, two_hbm))]
    loads_state.append(load(step_hbm, step_ref, 12))
    for h in range(2):
        for d, e in PAIRS:
            if h == 1 and d == 0:
                continue
            pl.semaphore_signal(barrier, inc=1, device_id=at(h, d, 0, e), device_id_type=pl.DeviceIdType.MESH)
    mod = rep * 2 + core
    primary = lax.rem(z, 4) == mod
    rank = sum(jnp.where(z == place, k, 0) for k, place in enumerate(ORDER))
    expected = 13
    for k, place in enumerate(ORDER):
        meets = jnp.logical_and(z != place, jnp.logical_or(primary, mod == place % 4))

        @pl.when(jnp.logical_and(meets, rank < k))
        def _():
            pl.semaphore_signal(
                barrier, inc=1, device_id=dev(x, y, place, core), device_id_type=pl.DeviceIdType.MESH
            )
        expected = expected + jnp.where(jnp.logical_and(meets, rank > k), 1, 0)

    glog_load.wait()
    glog = glog_ref[...]

    def pieces_of(start):
        cols = pl.ds(start if isinstance(start, int) else pl.multiple_of(start, 128), BLK)
        product = lax.dot_general(
            acts[:, cols], glog, (((0,), (0,)), ((), ())), preferred_element_type=F32
        ).astype(BF16)
        for zr in range(4):
            for ylo in range(2):
                lo = (zr * 2 + ylo) * UNIT
                yield (zr // 2) * 2 + ylo, zr % 2, product[lo:lo + UNIT]

    def remote(src, dst, send, recv, device):
        return pltpu.make_async_remote_copy(
            src_ref=src, dst_ref=dst, send_sem=send, recv_sem=recv,
            device_id=device, device_id_type=pl.DeviceIdType.MESH,
        )

    sent = []
    copy_a = {}

    def send_a(h, d, e):
        place = lax.rem(main[h] + d, 4) * 2 + lax.rem(core + e, 2)
        copy = remote(
            part.at[h, place], recv_a.at[h, d * 2 + e], sa.at[h, d * 2 + e], ra.at[h, d * 2 + e],
            at(h, d, 0, e),
        )
        copy.start()
        copy_a[h, d, e] = copy
        sent.append(copy)

    for k in range(4):
        loads_two[k].wait()
        for zg in range(2, 4):
            for py, pc, piece in pieces_of(k * 1536 + zg * BLK):
                lo = k * 96 + (zg - 2) * UNIT
                part[1, py * 2 + pc, lo:lo + UNIT] = piece
    pl.semaphore_wait(barrier, expected)
    for d, e in PAIRS:
        send_a(1, d, e)
    for d in STEPS:
        loads_one[d].wait()
        to = lax.rem(x + d, 4)
        for zg in range(2):
            for py, pc, piece in pieces_of(to * 1536 + zg * BLK):
                lo = py * 96 + zg * UNIT
                part[0, to * 2 + pc, lo:lo + UNIT] = piece
        for p, e in PAIRS:
            if p == d:
                send_a(0, p, e)

    for k, place in enumerate(ORDER):
        @pl.when(jnp.logical_and(primary, rank > k))
        def _():
            pl.semaphore_signal(
                ready.at[z // 4], inc=1, device_id=dev(x, y, place, core), device_id_type=pl.DeviceIdType.MESH
            )

    for copy in loads_state:
        copy.wait()
    half = pl.ds(pl.multiple_of(core * OWN, 8), OWN)
    state48[:, half, :] = state[...]
    state_copy = remote(state, state48.at[:, half, :], st_sem.at[0], st_sem.at[1], at(0, 0, 0, 1))
    state_copy.start()
    sent.append(state_copy)

    copy_b = {}
    for h in range(2):
        mine = main[h] * 2 + core
        for d, e in NEAR:
            copy_a[h, d, e].wait_recv()
        for d in (2, 1, 3, 0):
            to = lax.rem(cross[h] + d, 4)
            rows = pl.ds(pl.multiple_of(to * 96, 16), 96)
            total = part[h, mine, rows].astype(F32)
            for p, e in NEAR:
                total = total + recv_a[h, p * 2 + e, rows].astype(F32)
            acc[h, d] = total
            if d:
                copy = remote(acc.at[h, d], recv_b.at[h, d], sb.at[h, d], rb.at[h, d], at(h, 0, d, 0))
                copy.start()
                copy_b[h, d] = copy
                sent.append(copy)

    copy_c = []
    for h in range(2):
        for d in (1, 3, 2):
            copy_b[h, d].wait_recv()
        total = ((acc[h, 0] + recv_b[h, 1]) + recv_b[h, 3]) + recv_b[h, 2]
        for k in range(2):
            zg = h * 2 + k
            unit[zg] = total[k * UNIT:(k + 1) * UNIT]
            to = zg * 4 + mod
            dz = lax.rem(to + 16 - z, 16)
            copy = remote(unit.at[zg], recv_c.at[dz], sc.at[zg], rc.at[dz], dev(x, y, to, core))
            copy_c.append((copy, dz))
            rank_to = sum(jnp.where(to == place, k, 0) for k, place in enumerate(ORDER))

            @pl.when(rank < rank_to)
            def _():
                pl.semaphore_wait(ready.at[zg], 1)

            @pl.when(dz != 0)
            def _():
                copy.start()

            @pl.when(dz == 0)
            def _():
                own48[...] = unit[zg]

    count = step_ref[0].astype(F32)
    state_copy.wait_recv()
    other = pl.ds(pl.multiple_of((1 - core) * OWN, 8), OWN)

    def place(h, k):
        which = x * (1 - h) + y * h
        inner = y * (1 - h) + x * h
        return wnew.at[h, which * 2 + core, pl.ds(pl.multiple_of(inner * 96 + k * UNIT, 16), UNIT)]

    zg_me = z // 4
    spot = place(zg_me // 2, lax.rem(zg_me, 2))
    copy_z = {
        to: remote(spot, spot, sz.at[to], rz.at[zg_me], dev(x, y, to, core)) for to in range(16)
    }
    copy_d = [
        remote(own48.at[half], grad_own, sd.at[0], rd.at[0], at(1, 2, 0, 0)),
        remote(own48.at[other], grad_own, sd.at[1], rd.at[0], at(1, 0, 0, 1)),
        remote(own48.at[other], grad_own, sd.at[2], rd.at[0], at(1, 2, 0, 1)),
    ]

    @pl.when(primary)
    def _():
        for dz in range(1, 16):
            remote(recv_c.at[dz], recv_c.at[dz], sc.at[0], rc.at[dz], along_z(dz)).wait_recv()
        total = own48[...]
        for dz in range(1, 16):
            total = total + recv_c[dz]
        updated, _, _ = adam(total, state48[0], state48[1], state48[2], count)
        spot[...] = updated.astype(BF16)
        for to in (0, 1, 2, 3, 4, 15, 5, 14, 6, 13, 7, 12, 8, 11, 9, 10):
            @pl.when(z != to)
            def _():
                copy_z[to].start()
        own48[...] = total
        for copy in copy_d:
            copy.start()
        grad_own[...] = own48[half]

    copy_1 = {}
    for h in range(2):
        for k in range(2):
            zg = h * 2 + k

            @pl.when(z != zg * 4 + mod)
            def _():
                remote(place(h, k), place(h, k), sz.at[0], rz.at[zg], along_z(1)).wait_recv()
        rows = wnew.at[h, main[h] * 2 + core, pl.ds(pl.multiple_of(cross[h] * 96, 16), 96)]
        for d in (2, 1, 3):
            copy = remote(rows, rows, s1.at[h, d], r1.at[h, d], at(h, 0, d, 0))
            copy.start()
            copy_1[h, d] = copy
            sent.append(copy)

    copy_2 = {}
    copy_3 = {}

    def forward(h, d):
        lane = wnew.at[h, lax.rem(main[h] + d, 4) * 2 + core]
        copy = remote(lane, lane, s3.at[h, d], r3.at[h, d], at(h, 0, 0, 1))
        copy.start()
        copy_3[h, d] = copy
        sent.append(copy)

    for h in range(2):
        for d in (1, 3, 2):
            copy_1[h, d].wait_recv()
        block = wnew.at[h, main[h] * 2 + core]
        for d in (2, 1, 3):
            copy = remote(block, block, s2.at[h, d], r2.at[h, d], at(h, d, 0, 0))
            copy.start()
            copy_2[h, d] = copy
            sent.append(copy)
        forward(h, 0)

    @pl.when(jnp.logical_not(primary))
    def _():
        remote(grad_own, grad_own, sd.at[0], rd.at[0], at(1, 2, 0, 0)).wait_recv()

    grad_out[...] = grad_own[...]

    total = jnp.zeros((TOK, E), F32)
    for d in (0, 1, 3, 2):
        from_d = (4 - d) % 4
        if d:
            for h in range(2):
                copy_2[h, d].wait_recv()
                forward(h, from_d)
        copy_3[0, from_d].wait_recv()
        lane = lax.rem(x + from_d, 4)
        for zg in range(2):
            weights = [
                wnew[0, lane * 2 + zr % 2, ((zr // 2) * 2 + ylo) * 96 + zg * UNIT:((zr // 2) * 2 + ylo) * 96 + zg * UNIT + UNIT]
                for zr in range(4) for ylo in range(2)
            ]
            cols = pl.ds(pl.multiple_of(lane * 1536 + zg * BLK, 128), BLK)
            total = total + jnp.dot(acts[:, cols], jnp.concatenate(weights, axis=0), preferred_element_type=F32)
    for d in range(4):
        copy_3[1, d].wait_recv()
    for k in range(4):
        for zg in range(2):
            weights = [
                wnew[1, ((zr // 2) * 2 + ylo) * 2 + zr % 2, k * 96 + zg * UNIT:k * 96 + zg * UNIT + UNIT]
                for zr in range(4) for ylo in range(2)
            ]
            cols = pl.ds(k * 1536 + 768 + zg * BLK, BLK)
            total = total + jnp.dot(acts[:, cols], jnp.concatenate(weights, axis=0), preferred_element_type=F32)
    logits_out[...] = total.astype(BF16)

    for copy in sent:
        copy.wait_send()
    for copy, dz in copy_c:
        @pl.when(dz != 0)
        def _():
            copy.wait_send()

    @pl.when(primary)
    def _():
        for to in range(16):
            @pl.when(z != to)
            def _():
                copy_z[to].wait_send()
        for copy in copy_d:
            copy.wait_send()


def per_device(acts, grad_logits, master, moment_one, moment_two, step_count):
    vmem = pl.BlockSpec(memory_space=pltpu.VMEM)
    anywhere = pl.BlockSpec(memory_space=pl.ANY)
    dma = pltpu.SemaphoreType.DMA
    own = jax.ShapeDtypeStruct((OWN, E), F32)
    grad, logits = pl.pallas_call(
        kernel,
        out_shape=(own, jax.ShapeDtypeStruct((TOK, E), BF16)),
        in_specs=[
            anywhere, anywhere, anywhere, anywhere, anywhere, anywhere,
        ],
        out_specs=(vmem, vmem),
        scratch_shapes=[
            pltpu.SMEM((1,), jnp.int32),
            pltpu.VMEM((TOK, D), BF16),
            pltpu.VMEM((TOK, E), BF16),
            pltpu.VMEM((2, 8, BLK, E), BF16),
            pltpu.VMEM((2, 8, BLK, E), BF16),
            pltpu.VMEM((2, 4, 96, E), F32),
            pltpu.VMEM((2, 4, 96, E), F32),
            pltpu.VMEM((4, UNIT, E), F32),
            pltpu.VMEM((16, UNIT, E), F32),
            pltpu.VMEM((UNIT, E), F32),
            pltpu.VMEM((3, OWN, E), F32),
            pltpu.VMEM((3, UNIT, E), F32),
            pltpu.VMEM((OWN, E), F32),
            pltpu.VMEM((2, 8, BLK, E), BF16),
            dma((13,)), dma((2,)), pltpu.SemaphoreType.REGULAR((4,)),
            dma((2, 8)), dma((2, 8)),
            dma((2, 4)), dma((2, 4)),
            dma((4,)), dma((16,)),
            dma((3,)), dma((1,)),
            dma((16,)), dma((4,)),
            dma((2, 4)), dma((2, 4)),
            dma((2, 4)), dma((2, 4)),
            dma((2, 4)), dma((2, 4)),
        ],
        compiler_params=pltpu.CompilerParams(
            collective_id=0, has_side_effects=True, vmem_limit_bytes=60 * 1024 * 1024
        ),
        cost_estimate=pl.CostEstimate(flops=4 * TOK * D * E, bytes_accessed=3 * 1024 * 1024, transcendentals=0),
    )(step_count, acts, grad_logits, master, moment_one, moment_two)
    count = step_count[0].astype(F32)
    first = 0.9 * moment_one + (1.0 - 0.9) * grad
    second = 0.95 * moment_two + (1.0 - 0.95) * grad * grad
    first_hat = first / (1.0 - jnp.power(0.9, count))
    second_hat = second / (1.0 - jnp.power(0.95, count))
    updated = master - 0.01 * (first_hat / (jnp.sqrt(second_hat) + 1e-08) + 0.1 * master)
    return updated, first, second, logits


def solution(mesh):
    in_specs = (
        P(("seq", "rep"), None),
        P(("seq", "rep"), None),
        P("seq", None),
        P("seq", None),
        P("seq", None),
        P(),
    )
    out_specs = (P("seq", None), P("seq", None), P("seq", None), P(("seq", "rep"), None))
    return jax.shard_map(
        per_device, mesh=mesh, in_specs=in_specs, out_specs=out_specs, check_vma=False
    )
```

```python
import math

import jax
import jax.numpy as jnp
from jax import lax
from jax.experimental import pallas as pl
from jax.experimental.pallas import tpu as pltpu
from jax.sharding import PartitionSpec as P

D = 6144
E = 128
TOK = 256
OWN = 24
UNIT = 48
BLK = 384
F32 = jnp.float32
BF16 = jnp.bfloat16
PAIRS = ((2, 0), (2, 1), (1, 0), (3, 0), (1, 1), (3, 1), (0, 1))
STEPS = (2, 1, 3, 0)
CHUNKS = ((1, 0), (0, 1), (1, 1), (0, 0))
ORDER = (0, 1, 2, 3, 4, 5, 6, 7, 15, 14, 13, 8, 12, 9, 10, 11)
NEAR = ((0, 1), (1, 0), (3, 0), (1, 1), (3, 1), (2, 0), (2, 1))


def adam(grad, master, one, two, count):
    ones = jnp.ones((1, E), F32)
    first = 0.9 * one + (1.0 - 0.9) * grad
    second = 0.95 * two + (1.0 - 0.95) * grad * grad
    first_hat = first / (1.0 - jnp.exp(count * math.log(0.9) * ones))
    second_hat = second / (1.0 - jnp.exp(count * math.log(0.95) * ones))
    updated = master - 0.01 * (first_hat / (jnp.sqrt(second_hat) + 1e-08) + 0.1 * master)
    return updated, first, second


def kernel(
    step_hbm, acts_hbm, glog_hbm, master_hbm, one_hbm, two_hbm,
    grad_out, logits_out,
    step_ref, acts, glog_ref, part, recv_a, acc, recv_b, unit, recv_c, own48, state, state48, grad_own, wnew,
    load_sem, st_sem, ready, sa, ra, sb, rb, sc, rc, sd, rd, sz, rz, s1, r1, s2, r2, s3, r3,
):
    seq = lax.axis_index("seq")
    rep = lax.axis_index("rep")
    core = lax.rem(seq, 2)
    y = rep * 2 + lax.rem(seq // 2, 2)
    z = lax.rem(seq // 4, 16)
    x = seq // 64
    main = (x, y)
    cross = (y, x)

    def dev(px, py, pz, pc):
        return {"seq": ((px * 16 + pz) * 2 + lax.rem(py, 2)) * 2 + pc, "rep": py // 2}

    def at(h, dmain, dcross, dcore):
        dx, dy = (dmain, dcross) if h == 0 else (dcross, dmain)
        return dev(lax.rem(x + dx, 4), lax.rem(y + dy, 4), z, lax.rem(core + dcore, 2))

    def along_z(dz):
        return dev(x, y, lax.rem(z + dz, 16), core)

    def block(h, k, d):
        start = lax.rem(x + d, 4) * 1536 + (h * 2 + k) * BLK
        return pl.ds(pl.multiple_of(start, 128), BLK)

    def load(src, dst, number):
        copy = pltpu.make_async_copy(src, dst, load_sem.at[number])
        copy.start()
        return copy

    barrier = pltpu.get_barrier_semaphore()
    glog_load = load(glog_hbm, glog_ref, 16)
    loads = {}
    for h, k in CHUNKS:
        for d in STEPS:
            cols = block(h, k, d)
            loads[h, k, d] = load(acts_hbm.at[:, cols], acts.at[:, cols], (h * 2 + k) * 4 + d)
    loads_state = [load(ref, state.at[k], 17 + k) for k, ref in enumerate((master_hbm, one_hbm, two_hbm))]
    loads_state.append(load(step_hbm, step_ref, 20))
    for h in range(2):
        for d, e in PAIRS:
            if h == 1 and d == 0:
                continue
            pl.semaphore_signal(barrier, inc=1, device_id=at(h, d, 0, e), device_id_type=pl.DeviceIdType.MESH)
    mod = rep * 2 + core
    primary = lax.rem(z, 4) == mod
    rank = sum(jnp.where(z == place, k, 0) for k, place in enumerate(ORDER))
    expected = 13
    for k, place in enumerate(ORDER):
        meets = jnp.logical_and(z != place, jnp.logical_or(primary, mod == place % 4))

        @pl.when(jnp.logical_and(meets, rank < k))
        def _():
            pl.semaphore_signal(
                barrier, inc=1, device_id=dev(x, y, place, core), device_id_type=pl.DeviceIdType.MESH
            )
        expected = expected + jnp.where(jnp.logical_and(meets, rank > k), 1, 0)

    glog_load.wait()
    glog = glog_ref[...]

    def remote(src, dst, send, recv, device):
        return pltpu.make_async_remote_copy(
            src_ref=src, dst_ref=dst, send_sem=send, recv_sem=recv,
            device_id=device, device_id_type=pl.DeviceIdType.MESH,
        )

    sent = []
    copy_a = {}

    def send_a(h, k, d, e):
        q = h * 2 + k
        place = lax.rem(main[h] + d, 4) * 2 + lax.rem(core + e, 2)
        copy = remote(
            part.at[q, place], recv_a.at[q, d * 2 + e], sa.at[q, d * 2 + e], ra.at[q, d * 2 + e], at(h, d, 0, e)
        )
        copy.start()
        copy_a[h, k, d, e] = copy
        sent.append(copy)

    for h, k in CHUNKS:
        q = h * 2 + k
        for d in STEPS:
            to = lax.rem(x + d, 4)
            loads[h, k, d].wait()
            product = lax.dot_general(
                acts[:, block(h, k, d)], glog, (((0,), (0,)), ((), ())), preferred_element_type=F32
            ).astype(BF16)
            for zr in range(4):
                for ylo in range(2):
                    lo = (zr * 2 + ylo) * UNIT
                    py, pc = (zr // 2) * 2 + ylo, zr % 2
                    if h == 0:
                        part[q, to * 2 + pc, py * UNIT:(py + 1) * UNIT] = product[lo:lo + UNIT]
                    else:
                        part[q, py * 2 + pc, pl.ds(pl.multiple_of(to * UNIT, 16), UNIT)] = product[lo:lo + UNIT]
            if h == 0:
                for p, e in PAIRS:
                    if p == d:
                        send_a(h, k, p, e)
        if h == 1:
            if (h, k) == CHUNKS[0]:
                pl.semaphore_wait(barrier, expected)
            for d, e in PAIRS:
                send_a(h, k, d, e)
    for k, place in enumerate(ORDER):
        @pl.when(jnp.logical_and(primary, rank > k))
        def _():
            pl.semaphore_signal(
                ready.at[z // 4], inc=1, device_id=dev(x, y, place, core), device_id_type=pl.DeviceIdType.MESH
            )

    for copy in loads_state:
        copy.wait()
    half = pl.ds(pl.multiple_of(core * OWN, 8), OWN)
    state48[:, half, :] = state[...]
    state_copy = remote(state, state48.at[:, half, :], st_sem.at[0], st_sem.at[1], at(0, 0, 0, 1))
    state_copy.start()
    sent.append(state_copy)

    copy_b = {}
    for h, k in CHUNKS:
        q = h * 2 + k
        mine = main[h] * 2 + core
        for d, e in NEAR:
            copy_a[h, k, d, e].wait_recv()
        for d in (2, 1, 3, 0):
            to = lax.rem(cross[h] + d, 4)
            rows = pl.ds(pl.multiple_of(to * UNIT, 16), UNIT)
            total = part[q, mine, rows].astype(F32)
            for p, e in NEAR:
                total = total + recv_a[q, p * 2 + e, rows].astype(F32)
            acc[q, d] = total
            if d:
                copy = remote(acc.at[q, d], recv_b.at[q, d], sb.at[q, d], rb.at[q, d], at(h, 0, d, 0))
                copy.start()
                copy_b[h, k, d] = copy
                sent.append(copy)

    copy_c = []
    for h, k in CHUNKS:
        zg = h * 2 + k
        for d in (1, 3, 2):
            copy_b[h, k, d].wait_recv()
        unit[zg] = ((acc[zg, 0] + recv_b[zg, 1]) + recv_b[zg, 3]) + recv_b[zg, 2]
        to = zg * 4 + mod
        dz = lax.rem(to + 16 - z, 16)
        copy = remote(unit.at[zg], recv_c.at[dz], sc.at[zg], rc.at[dz], dev(x, y, to, core))
        copy_c.append((copy, dz))
        rank_to = sum(jnp.where(to == place, j, 0) for j, place in enumerate(ORDER))

        @pl.when(rank < rank_to)
        def _():
            pl.semaphore_wait(ready.at[zg], 1)

        @pl.when(dz != 0)
        def _():
            copy.start()

        @pl.when(dz == 0)
        def _():
            own48[...] = unit[zg]

    count = step_ref[0].astype(F32)
    state_copy.wait_recv()
    other = pl.ds(pl.multiple_of((1 - core) * OWN, 8), OWN)

    def place(zg):
        first = zg // 2 == 0
        which = jnp.where(first, x, y)
        inner = jnp.where(first, y, x)
        return wnew.at[zg, which * 2 + core, pl.ds(pl.multiple_of(inner * UNIT, 16), UNIT)]

    zg_me = z // 4
    spot = place(zg_me)
    copy_z = {
        to: remote(spot, spot, sz.at[to], rz.at[zg_me], dev(x, y, to, core)) for to in range(16)
    }
    copy_d = [
        remote(own48.at[half], grad_own, sd.at[0], rd.at[0], at(1, 2, 0, 0)),
        remote(own48.at[other], grad_own, sd.at[1], rd.at[0], at(1, 0, 0, 1)),
        remote(own48.at[other], grad_own, sd.at[2], rd.at[0], at(1, 2, 0, 1)),
    ]

    @pl.when(primary)
    def _():
        for dz in range(1, 16):
            remote(recv_c.at[dz], recv_c.at[dz], sc.at[0], rc.at[dz], along_z(dz)).wait_recv()
        total = own48[...]
        for dz in range(1, 16):
            total = total + recv_c[dz]
        updated, _, _ = adam(total, state48[0], state48[1], state48[2], count)
        spot[...] = updated.astype(BF16)
        for to in (0, 1, 2, 3, 4, 15, 5, 14, 6, 13, 7, 12, 8, 11, 9, 10):
            @pl.when(z != to)
            def _():
                copy_z[to].start()
        own48[...] = total
        for copy in copy_d:
            copy.start()
        grad_own[...] = own48[half]

    copy_1 = {}
    for h, k in CHUNKS:
        zg = h * 2 + k

        @pl.when(z != zg * 4 + mod)
        def _():
            remote(place(zg), place(zg), sz.at[0], rz.at[zg], along_z(1)).wait_recv()
        for d in (2, 1, 3):
            copy = remote(place(zg), place(zg), s1.at[zg, d], r1.at[zg, d], at(h, 0, d, 0))
            copy.start()
            copy_1[h, k, d] = copy
            sent.append(copy)

    copy_2 = {}
    copy_3 = {}

    def forward(h, k, d):
        q = h * 2 + k
        lane = wnew.at[q, lax.rem(main[h] + d, 4) * 2 + core]
        copy = remote(lane, lane, s3.at[q, d], r3.at[q, d], at(h, 0, 0, 1))
        copy.start()
        copy_3[h, k, d] = copy
        sent.append(copy)

    for h, k in CHUNKS:
        q = h * 2 + k
        for d in (1, 3, 2):
            copy_1[h, k, d].wait_recv()
        mine = wnew.at[q, main[h] * 2 + core]
        for d in (2, 1, 3):
            copy = remote(mine, mine, s2.at[q, d], r2.at[q, d], at(h, d, 0, 0))
            copy.start()
            copy_2[h, k, d] = copy
            sent.append(copy)
        forward(h, k, 0)

    @pl.when(jnp.logical_not(primary))
    def _():
        remote(grad_own, grad_own, sd.at[0], rd.at[0], at(1, 2, 0, 0)).wait_recv()

    grad_out[...] = grad_own[...]

    logits = jnp.zeros((TOK, E), F32)

    def apply(total, h, k):
        q = h * 2 + k
        for d in range(4):
            copy_3[h, k, d].wait_recv()
        for lane in range(4):
            weights = []
            for zr in range(4):
                for ylo in range(2):
                    py, pc = (zr // 2) * 2 + ylo, zr % 2
                    which, inner = (lane, py) if h == 0 else (py, lane)
                    weights.append(wnew[q, which * 2 + pc, inner * UNIT:(inner + 1) * UNIT])
            cols = pl.ds(lane * 1536 + q * BLK, BLK)
            total = total + jnp.dot(acts[:, cols], jnp.concatenate(weights, axis=0), preferred_element_type=F32)
        return total

    for number, (h, k) in enumerate(CHUNKS):
        for d in (1, 3, 2):
            copy_2[h, k, d].wait_recv()
            forward(h, k, 4 - d)
        if number:
            logits = apply(logits, *CHUNKS[number - 1])
    logits = apply(logits, *CHUNKS[-1])
    logits_out[...] = logits.astype(BF16)

    for copy in sent:
        copy.wait_send()
    for copy, dz in copy_c:
        @pl.when(dz != 0)
        def _():
            copy.wait_send()

    @pl.when(primary)
    def _():
        for to in range(16):
            @pl.when(z != to)
            def _():
                copy_z[to].wait_send()
        for copy in copy_d:
            copy.wait_send()


def per_device(acts, grad_logits, master, moment_one, moment_two, step_count):
    vmem = pl.BlockSpec(memory_space=pltpu.VMEM)
    anywhere = pl.BlockSpec(memory_space=pl.ANY)
    dma = pltpu.SemaphoreType.DMA
    own = jax.ShapeDtypeStruct((OWN, E), F32)
    grad, logits = pl.pallas_call(
        kernel,
        out_shape=(pltpu.VMEM((OWN, E), F32), pltpu.VMEM((TOK, E), BF16)),
        in_specs=[
            anywhere, anywhere, anywhere, anywhere, anywhere, anywhere,
        ],
        out_specs=(vmem, vmem),
        scratch_shapes=[
            pltpu.SMEM((1,), jnp.int32),
            pltpu.VMEM((TOK, D), BF16),
            pltpu.VMEM((TOK, E), BF16),
            pltpu.VMEM((4, 8, 4 * UNIT, E), BF16),
            pltpu.VMEM((4, 8, 4 * UNIT, E), BF16),
            pltpu.VMEM((4, 4, UNIT, E), F32),
            pltpu.VMEM((4, 4, UNIT, E), F32),
            pltpu.VMEM((4, UNIT, E), F32),
            pltpu.VMEM((16, UNIT, E), F32),
            pltpu.VMEM((UNIT, E), F32),
            pltpu.VMEM((3, OWN, E), F32),
            pltpu.VMEM((3, UNIT, E), F32),
            pltpu.VMEM((OWN, E), F32),
            pltpu.VMEM((4, 8, 4 * UNIT, E), BF16),
            dma((21,)), dma((2,)), pltpu.SemaphoreType.REGULAR((4,)),
            dma((4, 8)), dma((4, 8)),
            dma((4, 4)), dma((4, 4)),
            dma((4,)), dma((16,)),
            dma((3,)), dma((1,)),
            dma((16,)), dma((4,)),
            dma((4, 4)), dma((4, 4)),
            dma((4, 4)), dma((4, 4)),
            dma((4, 4)), dma((4, 4)),
        ],
        compiler_params=pltpu.CompilerParams(
            collective_id=0, has_side_effects=True, vmem_limit_bytes=60 * 1024 * 1024
        ),
        cost_estimate=pl.CostEstimate(flops=4 * TOK * D * E, bytes_accessed=3 * 1024 * 1024, transcendentals=0),
    )(step_count, acts, grad_logits, master, moment_one, moment_two)
    count = step_count[0].astype(F32)
    first = 0.9 * moment_one + (1.0 - 0.9) * grad
    second = 0.95 * moment_two + (1.0 - 0.95) * grad * grad
    first_hat = first / (1.0 - jnp.power(0.9, count))
    second_hat = second / (1.0 - jnp.power(0.95, count))
    updated = master - 0.01 * (first_hat / (jnp.sqrt(second_hat) + 1e-08) + 0.1 * master)
    return updated, first, second, logits


def solution(mesh):
    in_specs = (
        P(("seq", "rep"), None),
        P(("seq", "rep"), None),
        P("seq", None),
        P("seq", None),
        P("seq", None),
        P(),
    )
    out_specs = (P("seq", None), P("seq", None), P("seq", None), P(("seq", "rep"), None))
    return jax.shard_map(
        per_device, mesh=mesh, in_specs=in_specs, out_specs=out_specs, check_vma=False
    )
```

```python
import math

import jax
import jax.numpy as jnp
from jax import lax
from jax.experimental import pallas as pl
from jax.experimental.pallas import tpu as pltpu
from jax.sharding import PartitionSpec as P

D = 6144
E = 128
TOK = 256
OWN = 24
UNIT = 48
LEVELS = 32767.0
ROWS = 4 * UNIT
BLK = 384
F32 = jnp.float32
BF16 = jnp.bfloat16
PARTNERS = ((0, 2, 0), (0, 1, 0), (0, 3, 0), (1, 2, 0), (1, 1, 0), (1, 3, 0), (1, 2, 1), (1, 0, 1))
STEPS = (2, 1, 3, 0)
CHUNKS = ((1, 0), (0, 1), (1, 1), (0, 0))
GATHER = ((1, 0), (0, 1), (1, 1), (0, 0))
ORDER = (0, 1, 2, 3, 4, 5, 6, 7, 15, 14, 13, 8, 12, 9, 10, 11)
STEPS = (2, 1, 3, 0)
CHUNKS = ((1, 0), (0, 1), (1, 1), (0, 0))
GATHER = ((1, 0), (0, 1), (1, 1), (0, 0))
ORDER = (0, 1, 2, 3, 4, 5, 6, 7, 15, 14, 13, 8, 12, 9, 10, 11)
NEAR = ((0, 1), (1, 0), (3, 0), (1, 1), (3, 1), (2, 0), (2, 1))


def corrections(count):
    ones = jnp.ones((1, E), F32)
    return 1.0 - jnp.exp(count * math.log(0.9) * ones), 1.0 - jnp.exp(count * math.log(0.95) * ones)


def encode(total):
    most = jnp.max(jnp.abs(total), axis=0, keepdims=True)
    power = jnp.ceil(jnp.log2(jnp.maximum(most, 1e-30)))
    scaled = jnp.clip(total * (LEVELS * jnp.exp2(-power)), -LEVELS, LEVELS)
    codes = jnp.floor(scaled + 0.5).astype(jnp.int32).astype(jnp.int16)
    return codes, jnp.broadcast_to(power.astype(jnp.int32), (16, E)).astype(jnp.int16)


def decode_unit(powers):
    return jnp.exp2(powers.astype(jnp.int32).astype(F32)[:1]) * (1.0 / LEVELS)


def adam(grad, master, one, two, correction_one, correction_two):
    first = 0.9 * one + (1.0 - 0.9) * grad
    second = 0.95 * two + (1.0 - 0.95) * grad * grad
    first_hat = first / correction_one
    second_hat = second / correction_two
    updated = master - 0.01 * (first_hat / (jnp.sqrt(second_hat) + 1e-08) + 0.1 * master)
    return updated, first, second


def kernel(
    step_hbm, acts_hbm, glog_hbm, master_hbm, one_hbm, two_hbm,
    grad_out, logits_out,
    step_ref, acts, glog_ref, part, pair, code, recv_a, acc, recv_b, unit, recv_c, own48, state, state48, grad_own, wnew,
    load_sem, st_sem, ready, s0, r0, sa, ra, sb, rb, sc, rc, sd, rd, sz, rz, s1, r1, s2, r2, s3, r3,
):
    seq = lax.axis_index("seq")
    rep = lax.axis_index("rep")
    core = lax.rem(seq, 2)
    y = rep * 2 + lax.rem(seq // 2, 2)
    z = lax.rem(seq // 4, 16)
    x = seq // 64
    main = (x, y)
    cross = (y, x)

    def dev(px, py, pz, pc):
        return {"seq": ((px * 16 + pz) * 2 + lax.rem(py, 2)) * 2 + pc, "rep": py // 2}

    def at(h, dmain, dcross, dcore):
        dx, dy = (dmain, dcross) if h == 0 else (dcross, dmain)
        return dev(lax.rem(x + dx, 4), lax.rem(y + dy, 4), z, lax.rem(core + dcore, 2))

    def along_z(dz):
        return dev(x, y, lax.rem(z + dz, 16), core)

    def load(src, dst, number):
        copy = pltpu.make_async_copy(src, dst, load_sem.at[number])
        copy.start()
        return copy

    barrier = pltpu.get_barrier_semaphore()
    for h, d, e in PARTNERS:
        pl.semaphore_signal(barrier, inc=1, device_id=at(h, d, 0, e), device_id_type=pl.DeviceIdType.MESH)
    glog_load = load(glog_hbm, glog_ref, 16)
    loads = []
    for k in range(4):
        cols = pl.ds(k * 1536, 1536)
        loads.append(load(acts_hbm.at[:, cols], acts.at[:, cols], k))
    loads_state = [load(ref, state.at[k], 17 + k) for k, ref in enumerate((master_hbm, one_hbm, two_hbm))]
    loads_state.append(load(step_hbm, step_ref, 20))
    mod = rep * 2 + core
    primary = lax.rem(z, 4) == mod
    rank = sum(jnp.where(z == place, k, 0) for k, place in enumerate(ORDER))
    expected = len(PARTNERS)
    for k, place in enumerate(ORDER):
        meets = jnp.logical_and(z != place, jnp.logical_or(primary, mod == place % 4))

        @pl.when(jnp.logical_and(meets, rank < k))
        def _():
            pl.semaphore_signal(
                barrier, inc=1, device_id=dev(x, y, place, core), device_id_type=pl.DeviceIdType.MESH
            )
        expected = expected + jnp.where(jnp.logical_and(meets, rank > k), 1, 0)

    glog_load.wait()
    glog = glog_ref[...]

    def remote(src, dst, send, recv, device):
        return pltpu.make_async_remote_copy(
            src_ref=src, dst_ref=dst, send_sem=send, recv_sem=recv,
            device_id=device, device_id_type=pl.DeviceIdType.MESH,
        )

    for copy in loads:
        copy.wait()
    for h, k in CHUNKS:
        q = h * 2 + k
        for px in range(4):
            cols = pl.ds(px * 1536 + q * BLK, BLK)
            product = lax.dot_general(
                glog, acts[:, cols], (((0,), (0,)), ((), ())), preferred_element_type=F32
            ).T.astype(BF16)
            for zr in range(4):
                for ylo in range(2):
                    lo = (zr * 2 + ylo) * UNIT
                    py, pc = (zr // 2) * 2 + ylo, zr % 2
                    which, inner = (px, py) if h == 0 else (py, px)
                    part[q, which * 2 + pc, inner * UNIT:(inner + 1) * UNIT] = product[lo:lo + UNIT]

    sent = []
    copy_0 = {}
    copy_a = {}
    pl.semaphore_wait(barrier, expected)
    for h, k in CHUNKS:
        q = h * 2 + k
        for d in STEPS:
            lane = lax.rem(main[h] + d, 4)
            copy = remote(
                part.at[q, lane * 2 + 1 - core], pair.at[q, d], s0.at[q, d], r0.at[q, d], at(h, 0, 0, 1)
            )
            copy.start()
            copy_0[h, k, d] = copy
            sent.append(copy)
    for h, k in CHUNKS:
        q = h * 2 + k
        for d in STEPS:
            copy_0[h, k, d].wait_recv()
        for d in (2, 1, 3):
            total = part[q, lax.rem(main[h] + d, 4) * 2 + core].astype(F32) + pair[q, d].astype(F32)
            code[q, d, :ROWS], code[q, d, ROWS:] = encode(total)
        for d in (2, 1, 3):
            copy = remote(code.at[q, d], recv_a.at[q, d], sa.at[q, d], ra.at[q, d], at(h, d, 0, 0))
            copy.start()
            copy_a[h, k, d] = copy
            sent.append(copy)
    for k, place in enumerate(ORDER):
        @pl.when(jnp.logical_and(primary, rank > k))
        def _():
            pl.semaphore_signal(
                ready.at[z // 4], inc=1, device_id=dev(x, y, place, core), device_id_type=pl.DeviceIdType.MESH
            )

    for copy in loads_state:
        copy.wait()
    half = pl.ds(pl.multiple_of(core * OWN, 8), OWN)
    state48[:, half, :] = state[...]
    state_copy = remote(state, state48.at[:, half, :], st_sem.at[0], st_sem.at[1], at(0, 0, 0, 1))
    state_copy.start()
    sent.append(state_copy)

    copy_b = {}
    for h, k in CHUNKS:
        q = h * 2 + k
        mine = main[h] * 2 + core
        for d in (1, 3, 2):
            copy_a[h, k, d].wait_recv()
        units = {d: decode_unit(recv_a[q, d, ROWS:]) for d in (1, 3, 2)}
        for d in (2, 1, 3, 0):
            to = lax.rem(cross[h] + d, 4)
            rows = pl.ds(pl.multiple_of(to * UNIT, 16), UNIT)
            total = part[q, mine, rows].astype(F32) + pair[q, 0, rows].astype(F32)
            for p in (1, 3, 2):
                total = total + recv_a[q, p, rows].astype(jnp.int32).astype(F32) * units[p]
            acc[q, d] = total
        for d in (2, 1, 3, 0):
            if d:
                copy = remote(acc.at[q, d], recv_b.at[q, d], sb.at[q, d], rb.at[q, d], at(h, 0, d, 0))
                copy.start()
                copy_b[h, k, d] = copy
                sent.append(copy)

    copy_c = []
    for h, k in CHUNKS:
        zg = h * 2 + k
        for d in (1, 3, 2):
            copy_b[h, k, d].wait_recv()
        unit[zg] = ((acc[zg, 0] + recv_b[zg, 1]) + recv_b[zg, 3]) + recv_b[zg, 2]
        to = zg * 4 + mod
        dz = lax.rem(to + 16 - z, 16)
        copy = remote(unit.at[zg], recv_c.at[z], sc.at[zg], rc.at[z], dev(x, y, to, core))
        copy_c.append((copy, dz))
        rank_to = sum(jnp.where(to == place, j, 0) for j, place in enumerate(ORDER))

        @pl.when(rank < rank_to)
        def _():
            pl.semaphore_wait(ready.at[zg], 1)

        @pl.when(dz != 0)
        def _():
            copy.start()

        @pl.when(dz == 0)
        def _():
            own48[...] = unit[zg]

    scales = corrections(step_ref[0].astype(F32))
    state_copy.wait_recv()
    for copy in sent:
        copy.wait_send()
    sent = []
    other = pl.ds(pl.multiple_of((1 - core) * OWN, 8), OWN)

    def place(zg):
        first = zg // 2 == 0
        which = jnp.where(first, x, y)
        inner = jnp.where(first, y, x)
        return wnew.at[zg, which * 2 + core, pl.ds(pl.multiple_of(inner * UNIT, 16), UNIT)]

    zg_me = z // 4
    spot = place(zg_me)
    copy_z = {
        to: remote(spot, spot, sz.at[to], rz.at[zg_me], dev(x, y, to, core)) for to in range(16)
    }
    copy_d = [
        remote(own48.at[half], grad_own, sd.at[0], rd.at[0], at(1, 2, 0, 0)),
        remote(own48.at[other], grad_own, sd.at[1], rd.at[0], at(1, 0, 0, 1)),
        remote(own48.at[other], grad_own, sd.at[2], rd.at[0], at(1, 2, 0, 1)),
    ]

    @pl.when(primary)
    def _():
        recv_c[z] = own48[...]
        total = jnp.zeros((UNIT, E), F32)
        for place in ORDER:
            @pl.when(z != place)
            def _():
                remote(recv_c.at[place], recv_c.at[place], sc.at[0], rc.at[place], along_z(1)).wait_recv()
            total = total + recv_c[place]
        updated, _, _ = adam(total, state48[0], state48[1], state48[2], *scales)
        spot[...] = updated.astype(BF16)
        for to in (0, 1, 2, 3, 4, 15, 5, 14, 6, 13, 7, 12, 8, 11, 9, 10):
            @pl.when(z != to)
            def _():
                copy_z[to].start()
        own48[...] = total
        for copy in copy_d:
            copy.start()
        grad_own[...] = own48[half]

    copy_1 = {}
    for h, k in GATHER:
        zg = h * 2 + k

        @pl.when(z != zg * 4 + mod)
        def _():
            remote(place(zg), place(zg), sz.at[0], rz.at[zg], along_z(1)).wait_recv()
        for d in (2, 1, 3):
            copy = remote(place(zg), place(zg), s1.at[zg, d], r1.at[zg, d], at(h, 0, d, 0))
            copy.start()
            copy_1[h, k, d] = copy
            sent.append(copy)

    for copy, dz in copy_c:
        @pl.when(dz != 0)
        def _():
            copy.wait_send()

    copy_2 = {}
    copy_3 = {}

    def forward(h, k, d):
        q = h * 2 + k
        lane = wnew.at[q, lax.rem(main[h] + d, 4) * 2 + core]
        copy = remote(lane, lane, s3.at[q, d], r3.at[q, d], at(h, 0, 0, 1))
        copy.start()
        copy_3[h, k, d] = copy
        sent.append(copy)

    for h, k in GATHER:
        q = h * 2 + k
        for d in (1, 3, 2):
            copy_1[h, k, d].wait_recv()
        mine = wnew.at[q, main[h] * 2 + core]
        for d in (2, 1, 3):
            copy = remote(mine, mine, s2.at[q, d], r2.at[q, d], at(h, d, 0, 0))
            copy.start()
            copy_2[h, k, d] = copy
            sent.append(copy)
        forward(h, k, 0)

    @pl.when(jnp.logical_not(primary))
    def _():
        remote(grad_own, grad_own, sd.at[0], rd.at[0], at(1, 2, 0, 0)).wait_recv()

    grad_out[...] = grad_own[...]

    @pl.when(primary)
    def _():
        for to in range(16):
            @pl.when(z != to)
            def _():
                copy_z[to].wait_send()
        for copy in copy_d:
            copy.wait_send()

    logits = jnp.zeros((TOK, E), F32)

    def apply(total, h, k):
        q = h * 2 + k
        for d in range(4):
            copy_3[h, k, d].wait_recv()
        for lane in range(4):
            weights = []
            for zr in range(4):
                for ylo in range(2):
                    py, pc = (zr // 2) * 2 + ylo, zr % 2
                    which, inner = (lane, py) if h == 0 else (py, lane)
                    weights.append(wnew[q, which * 2 + pc, inner * UNIT:(inner + 1) * UNIT])
            cols = pl.ds(lane * 1536 + q * BLK, BLK)
            total = total + jnp.dot(acts[:, cols], jnp.concatenate(weights, axis=0), preferred_element_type=F32)
        return total

    for number, (h, k) in enumerate(GATHER):
        for d in (1, 3, 2):
            copy_2[h, k, d].wait_recv()
            forward(h, k, 4 - d)
        if number:
            logits = apply(logits, *GATHER[number - 1])
    logits = apply(logits, *GATHER[-1])
    logits_out[...] = logits.astype(BF16)

    for copy in sent:
        copy.wait_send()


def per_device(acts, grad_logits, master, moment_one, moment_two, step_count):
    vmem = pl.BlockSpec(memory_space=pltpu.VMEM)
    anywhere = pl.BlockSpec(memory_space=pl.ANY)
    dma = pltpu.SemaphoreType.DMA
    own = jax.ShapeDtypeStruct((OWN, E), F32)
    grad, logits = pl.pallas_call(
        kernel,
        out_shape=(pltpu.VMEM((OWN, E), F32), pltpu.VMEM((TOK, E), BF16)),
        in_specs=[
            anywhere, anywhere, anywhere, anywhere, anywhere, anywhere,
        ],
        out_specs=(vmem, vmem),
        scratch_shapes=[
            pltpu.SMEM((1,), jnp.int32),
            pltpu.VMEM((TOK, D), BF16),
            pltpu.VMEM((TOK, E), BF16),
            pltpu.VMEM((4, 8, ROWS, E), BF16),
            pltpu.VMEM((4, 4, ROWS, E), BF16),
            pltpu.VMEM((4, 4, ROWS + 16, E), jnp.int16),
            pltpu.VMEM((4, 4, ROWS + 16, E), jnp.int16),
            pltpu.VMEM((4, 4, UNIT, E), F32),
            pltpu.VMEM((4, 4, UNIT, E), F32),
            pltpu.VMEM((4, UNIT, E), F32),
            pltpu.VMEM((16, UNIT, E), F32),
            pltpu.VMEM((UNIT, E), F32),
            pltpu.VMEM((3, OWN, E), F32),
            pltpu.VMEM((3, UNIT, E), F32),
            pltpu.VMEM((OWN, E), F32),
            pltpu.VMEM((4, 8, 4 * UNIT, E), BF16),
            dma((21,)), dma((2,)), pltpu.SemaphoreType.REGULAR((4,)),
            dma((4, 4)), dma((4, 4)),
            dma((4, 4)), dma((4, 4)),
            dma((4, 4)), dma((4, 4)),
            dma((4,)), dma((16,)),
            dma((3,)), dma((1,)),
            dma((16,)), dma((4,)),
            dma((4, 4)), dma((4, 4)),
            dma((4, 4)), dma((4, 4)),
            dma((4, 4)), dma((4, 4)),
        ],
        compiler_params=pltpu.CompilerParams(
            collective_id=0, has_side_effects=True, vmem_limit_bytes=60 * 1024 * 1024
        ),
        cost_estimate=pl.CostEstimate(flops=4 * TOK * D * E, bytes_accessed=3 * 1024 * 1024, transcendentals=0),
    )(step_count, acts, grad_logits, master, moment_one, moment_two)
    count = step_count[0].astype(F32)
    first = 0.9 * moment_one + (1.0 - 0.9) * grad
    second = 0.95 * moment_two + (1.0 - 0.95) * grad * grad
    first_hat = first / (1.0 - jnp.power(0.9, count))
    second_hat = second / (1.0 - jnp.power(0.95, count))
    updated = master - 0.01 * (first_hat / (jnp.sqrt(second_hat) + 1e-08) + 0.1 * master)
    return updated, first, second, logits


def solution(mesh):
    in_specs = (
        P(("seq", "rep"), None),
        P(("seq", "rep"), None),
        P("seq", None),
        P("seq", None),
        P("seq", None),
        P(),
    )
    out_specs = (P("seq", None), P("seq", None), P("seq", None), P(("seq", "rep"), None))
    return jax.shard_map(
        per_device, mesh=mesh, in_specs=in_specs, out_specs=out_specs, check_vma=False
    )
```

```python
import math

import jax
import jax.numpy as jnp
from jax import lax
from jax.experimental import pallas as pl
from jax.experimental.pallas import tpu as pltpu
from jax.sharding import PartitionSpec as P

D = 6144
E = 128
TOK = 256
OWN = 24
UNIT = 48
LEVELS = 32767.0
ROWS = 4 * UNIT
BLK = 384
F32 = jnp.float32
BF16 = jnp.bfloat16
PARTNERS = ((0, 2, 0), (0, 1, 0), (0, 3, 0), (1, 2, 0), (1, 1, 0), (1, 3, 0), (1, 2, 1), (1, 0, 1))
STEPS = (2, 1, 3, 0)
CHUNKS = ((1, 0), (0, 1), (1, 1), (0, 0))
GATHER = ((1, 0), (0, 1), (1, 1), (0, 0))
ORDER = (0, 1, 2, 3, 4, 5, 6, 7, 15, 14, 13, 8, 12, 9, 10, 11)
STEPS = (2, 1, 3, 0)
CHUNKS = ((1, 0), (0, 1), (1, 1), (0, 0))
GATHER = ((1, 0), (0, 1), (1, 1), (0, 0))
ORDER = (0, 1, 2, 3, 4, 5, 6, 7, 15, 14, 13, 8, 12, 9, 10, 11)
NEAR = ((0, 1), (1, 0), (3, 0), (1, 1), (3, 1), (2, 0), (2, 1))


def corrections(count):
    ones = jnp.ones((1, E), F32)
    return 1.0 - jnp.exp(count * math.log(0.9) * ones), 1.0 - jnp.exp(count * math.log(0.95) * ones)


def encode(total):
    most = jnp.max(jnp.abs(total), axis=0, keepdims=True)
    power = jnp.ceil(jnp.log2(jnp.maximum(most, 1e-30)))
    scaled = jnp.clip(total * (LEVELS * jnp.exp2(-power)), -LEVELS, LEVELS)
    codes = jnp.floor(scaled + 0.5).astype(jnp.int32).astype(jnp.int16)
    return codes, jnp.broadcast_to(power.astype(jnp.int32), (16, E)).astype(jnp.int16)


def decode_unit(powers):
    return jnp.exp2(powers.astype(jnp.int32).astype(F32)[:1]) * (1.0 / LEVELS)


def adam(grad, master, one, two, correction_one, correction_two):
    first = 0.9 * one + (1.0 - 0.9) * grad
    second = 0.95 * two + (1.0 - 0.95) * grad * grad
    first_hat = first / correction_one
    second_hat = second / correction_two
    updated = master - 0.01 * (first_hat / (jnp.sqrt(second_hat) + 1e-08) + 0.1 * master)
    return updated, first, second


def kernel(
    step_hbm, acts_hbm, glog_hbm, master_hbm, one_hbm, two_hbm,
    grad_out, logits_out,
    step_ref, acts, glog_ref, part, pair, code, recv_a, acc, recv_b, unit, recv_c, own48, state, state48, grad_own, wnew,
    load_sem, st_sem, ready, s0, r0, sa, ra, sb, rb, sc, rc, sd, rd, sz, rz, s1, r1, s2, r2, s3, r3,
):
    seq = lax.axis_index("seq")
    rep = lax.axis_index("rep")
    core = lax.rem(seq, 2)
    y = rep * 2 + lax.rem(seq // 2, 2)
    z = lax.rem(seq // 4, 16)
    x = seq // 64
    main = (x, y)
    cross = (y, x)

    def dev(px, py, pz, pc):
        return {"seq": ((px * 16 + pz) * 2 + lax.rem(py, 2)) * 2 + pc, "rep": py // 2}

    def at(h, dmain, dcross, dcore):
        dx, dy = (dmain, dcross) if h == 0 else (dcross, dmain)
        return dev(lax.rem(x + dx, 4), lax.rem(y + dy, 4), z, lax.rem(core + dcore, 2))

    def along_z(dz):
        return dev(x, y, lax.rem(z + dz, 16), core)

    def load(src, dst, number):
        copy = pltpu.make_async_copy(src, dst, load_sem.at[number])
        copy.start()
        return copy

    barrier = pltpu.get_barrier_semaphore()
    for h, d, e in PARTNERS:
        pl.semaphore_signal(barrier, inc=1, device_id=at(h, d, 0, e), device_id_type=pl.DeviceIdType.MESH)
    glog_load = load(glog_hbm, glog_ref, 0)
    for k in range(4):
        cols = pl.ds(k * 1536, 1536)
        load(acts_hbm.at[:, cols], acts.at[:, cols], 1)
    for k, ref in enumerate((master_hbm, one_hbm, two_hbm)):
        load(ref, state.at[k], 2)
    step_load = load(step_hbm, step_ref, 3)
    mod = rep * 2 + core
    primary = lax.rem(z, 4) == mod
    rank = sum(jnp.where(z == place, k, 0) for k, place in enumerate(ORDER))
    expected = len(PARTNERS)
    for k, place in enumerate(ORDER):
        meets = jnp.logical_and(z != place, jnp.logical_or(primary, mod == place % 4))

        @pl.when(jnp.logical_and(meets, rank < k))
        def _():
            pl.semaphore_signal(
                barrier, inc=1, device_id=dev(x, y, place, core), device_id_type=pl.DeviceIdType.MESH
            )
        expected = expected + jnp.where(jnp.logical_and(meets, rank > k), 1, 0)

    glog_load.wait()
    glog = glog_ref[...]

    def remote(src, dst, send, recv, device):
        return pltpu.make_async_remote_copy(
            src_ref=src, dst_ref=dst, send_sem=send, recv_sem=recv,
            device_id=device, device_id_type=pl.DeviceIdType.MESH,
        )

    def arrived(ref, sem):
        remote(ref, ref, sem, sem, along_z(1)).wait_recv()

    def left(ref, sem):
        remote(ref, ref, sem, sem, along_z(1)).wait_send()

    pltpu.make_async_copy(acts_hbm, acts, load_sem.at[1]).wait()
    for h, k in CHUNKS:
        q = h * 2 + k
        for px in range(4):
            cols = pl.ds(px * 1536 + q * BLK, BLK)
            product = lax.dot_general(
                glog, acts[:, cols], (((0,), (0,)), ((), ())), preferred_element_type=F32
            ).T.astype(BF16)
            for zr in range(4):
                for ylo in range(2):
                    lo = (zr * 2 + ylo) * UNIT
                    py, pc = (zr // 2) * 2 + ylo, zr % 2
                    which, inner = (px, py) if h == 0 else (py, px)
                    part[q, which * 2 + pc, inner * UNIT:(inner + 1) * UNIT] = product[lo:lo + UNIT]

    pl.semaphore_wait(barrier, expected)
    for h, k in CHUNKS:
        q = h * 2 + k
        for d in STEPS:
            lane = lax.rem(main[h] + d, 4)
            copy = remote(
                part.at[q, lane * 2 + 1 - core], pair.at[q, d], s0.at[0], r0.at[q], at(h, 0, 0, 1)
            )
            copy.start()
    for h, k in CHUNKS:
        q = h * 2 + k
        arrived(pair.at[q], r0.at[q])
        for d in (2, 1, 3):
            total = part[q, lax.rem(main[h] + d, 4) * 2 + core].astype(F32) + pair[q, d].astype(F32)
            code[q, d, :ROWS], code[q, d, ROWS:] = encode(total)
        for d in (2, 1, 3):
            copy = remote(code.at[q, d], recv_a.at[q, d], sa.at[0], ra.at[q], at(h, d, 0, 0))
            copy.start()
    for k, place in enumerate(ORDER):
        @pl.when(jnp.logical_and(primary, rank > k))
        def _():
            pl.semaphore_signal(
                ready.at[z // 4], inc=1, device_id=dev(x, y, place, core), device_id_type=pl.DeviceIdType.MESH
            )

    step_load.wait()
    pltpu.make_async_copy(state, state, load_sem.at[2]).wait()
    half = pl.ds(pl.multiple_of(core * OWN, 8), OWN)
    state48[:, half, :] = state[...]
    state_copy = remote(state, state48.at[:, half, :], st_sem.at[0], st_sem.at[1], at(0, 0, 0, 1))
    state_copy.start()

    for h, k in CHUNKS:
        q = h * 2 + k
        mine = main[h] * 2 + core
        arrived(recv_a.at[q, 1:4], ra.at[q])
        units = {d: decode_unit(recv_a[q, d, ROWS:]) for d in (1, 3, 2)}
        for d in (2, 1, 3, 0):
            to = lax.rem(cross[h] + d, 4)
            rows = pl.ds(pl.multiple_of(to * UNIT, 16), UNIT)
            total = part[q, mine, rows].astype(F32) + pair[q, 0, rows].astype(F32)
            for p in (1, 3, 2):
                total = total + recv_a[q, p, rows].astype(jnp.int32).astype(F32) * units[p]
            acc[q, d] = total
        for d in (2, 1, 3, 0):
            if d:
                copy = remote(acc.at[q, d], recv_b.at[q, d], sb.at[0], rb.at[q], at(h, 0, d, 0))
                copy.start()

    copy_c = []
    for h, k in CHUNKS:
        zg = h * 2 + k
        arrived(recv_b.at[zg, 1:4], rb.at[zg])
        unit[zg] = ((acc[zg, 0] + recv_b[zg, 1]) + recv_b[zg, 3]) + recv_b[zg, 2]
        to = zg * 4 + mod
        dz = lax.rem(to + 16 - z, 16)
        copy = remote(unit.at[zg], recv_c.at[z], sc.at[zg], rc.at[0], dev(x, y, to, core))
        copy_c.append((copy, dz))
        rank_to = sum(jnp.where(to == place, j, 0) for j, place in enumerate(ORDER))

        @pl.when(rank < rank_to)
        def _():
            pl.semaphore_wait(ready.at[zg], 1)

        @pl.when(dz != 0)
        def _():
            copy.start()

        @pl.when(dz == 0)
        def _():
            own48[...] = unit[zg]

    scales = corrections(step_ref[0].astype(F32))
    state_copy.wait_recv()
    state_copy.wait_send()
    left(pair, s0.at[0])
    left(code.at[0:3], sa.at[0])
    left(acc.at[0:3], sb.at[0])
    other = pl.ds(pl.multiple_of((1 - core) * OWN, 8), OWN)

    def place(zg):
        first = zg // 2 == 0
        which = jnp.where(first, x, y)
        inner = jnp.where(first, y, x)
        return wnew.at[zg, which * 2 + core, pl.ds(pl.multiple_of(inner * UNIT, 16), UNIT)]

    zg_me = z // 4
    spot = place(zg_me)
    copy_z = {
        to: remote(spot, spot, sz.at[0], rz.at[zg_me], dev(x, y, to, core)) for to in range(16)
    }
    copy_d = [
        remote(own48.at[half], grad_own, sd.at[0], rd.at[0], at(1, 2, 0, 0)),
        remote(own48.at[other], grad_own, sd.at[0], rd.at[0], at(1, 0, 0, 1)),
        remote(own48.at[other], grad_own, sd.at[0], rd.at[0], at(1, 2, 0, 1)),
    ]

    @pl.when(primary)
    def _():
        recv_c[z] = own48[...]
        arrived(recv_c.at[0:15], rc.at[0])
        total = recv_c[0]
        for place in range(1, 16):
            total = total + recv_c[place]
        updated, _, _ = adam(total, state48[0], state48[1], state48[2], *scales)
        spot[...] = updated.astype(BF16)
        for to in (0, 1, 2, 3, 4, 15, 5, 14, 6, 13, 7, 12, 8, 11, 9, 10):
            @pl.when(z != to)
            def _():
                copy_z[to].start()
        own48[...] = total
        for copy in copy_d:
            copy.start()
        grad_own[...] = own48[half]

    for h, k in GATHER:
        zg = h * 2 + k

        @pl.when(z != zg * 4 + mod)
        def _():
            remote(place(zg), place(zg), sz.at[0], rz.at[zg], along_z(1)).wait_recv()
        for d in (2, 1, 3):
            copy = remote(place(zg), place(zg), s1.at[0], r1.at[zg], at(h, 0, d, 0))
            copy.start()

    for copy, dz in copy_c:
        @pl.when(dz != 0)
        def _():
            copy.wait_send()

    copy_2 = {}

    def forward(h, k, d):
        q = h * 2 + k
        lane = wnew.at[q, lax.rem(main[h] + d, 4) * 2 + core]
        copy = remote(lane, lane, s3.at[0], r3.at[q], at(h, 0, 0, 1))
        copy.start()

    for h, k in GATHER:
        q = h * 2 + k
        arrived(wnew.at[q, 0, 0:3 * UNIT], r1.at[q])
        mine = wnew.at[q, main[h] * 2 + core]
        for d in (2, 1, 3):
            copy = remote(mine, mine, s2.at[0], r2.at[q, d - 1], at(h, d, 0, 0))
            copy.start()
            copy_2[h, k, d] = copy
        forward(h, k, 0)

    @pl.when(jnp.logical_not(primary))
    def _():
        remote(grad_own, grad_own, sd.at[0], rd.at[0], at(1, 2, 0, 0)).wait_recv()

    grad_out[...] = grad_own[...]

    @pl.when(primary)
    def _():
        left(acts.at[0:240, 0:BLK], sz.at[0])
        left(state, sd.at[0])

    logits = jnp.zeros((TOK, E), F32)

    def apply(total, h, k):
        q = h * 2 + k
        arrived(wnew.at[q, 0:4], r3.at[q])
        for lane in range(4):
            weights = []
            for zr in range(4):
                for ylo in range(2):
                    py, pc = (zr // 2) * 2 + ylo, zr % 2
                    which, inner = (lane, py) if h == 0 else (py, lane)
                    weights.append(wnew[q, which * 2 + pc, inner * UNIT:(inner + 1) * UNIT])
            cols = pl.ds(lane * 1536 + q * BLK, BLK)
            total = total + jnp.dot(acts[:, cols], jnp.concatenate(weights, axis=0), preferred_element_type=F32)
        return total

    for number, (h, k) in enumerate(GATHER):
        for d in (1, 3, 2):
            copy_2[h, k, d].wait_recv()
            forward(h, k, 4 - d)
        if number:
            logits = apply(logits, *GATHER[number - 1])
    logits = apply(logits, *GATHER[-1])
    logits_out[...] = logits.astype(BF16)

    left(wnew.at[0, 0:3], s1.at[0])
    left(wnew.at[0:3, 0:4], s2.at[0])
    left(wnew.at[0:2], s3.at[0])


def per_device(acts, grad_logits, master, moment_one, moment_two, step_count):
    vmem = pl.BlockSpec(memory_space=pltpu.VMEM)
    anywhere = pl.BlockSpec(memory_space=pl.ANY)
    dma = pltpu.SemaphoreType.DMA
    own = jax.ShapeDtypeStruct((OWN, E), F32)
    grad, logits = pl.pallas_call(
        kernel,
        out_shape=(pltpu.VMEM((OWN, E), F32), pltpu.VMEM((TOK, E), BF16)),
        in_specs=[
            anywhere, anywhere, anywhere, anywhere, anywhere, anywhere,
        ],
        out_specs=(vmem, vmem),
        scratch_shapes=[
            pltpu.SMEM((1,), jnp.int32),
            pltpu.VMEM((TOK, D), BF16),
            pltpu.VMEM((TOK, E), BF16),
            pltpu.VMEM((4, 8, ROWS, E), BF16),
            pltpu.VMEM((4, 4, ROWS, E), BF16),
            pltpu.VMEM((4, 4, ROWS + 16, E), jnp.int16),
            pltpu.VMEM((4, 4, ROWS + 16, E), jnp.int16),
            pltpu.VMEM((4, 4, UNIT, E), F32),
            pltpu.VMEM((4, 4, UNIT, E), F32),
            pltpu.VMEM((4, UNIT, E), F32),
            pltpu.VMEM((16, UNIT, E), F32),
            pltpu.VMEM((UNIT, E), F32),
            pltpu.VMEM((3, OWN, E), F32),
            pltpu.VMEM((3, UNIT, E), F32),
            pltpu.VMEM((OWN, E), F32),
            pltpu.VMEM((4, 8, 4 * UNIT, E), BF16),
            dma((4,)), dma((2,)), pltpu.SemaphoreType.REGULAR((4,)),
            dma((1,)), dma((4,)),
            dma((1,)), dma((4,)),
            dma((1,)), dma((4,)),
            dma((4,)), dma((1,)),
            dma((1,)), dma((1,)),
            dma((1,)), dma((4,)),
            dma((1,)), dma((4,)),
            dma((1,)), dma((4, 3)),
            dma((1,)), dma((4,)),
        ],
        compiler_params=pltpu.CompilerParams(
            collective_id=0, has_side_effects=True, vmem_limit_bytes=60 * 1024 * 1024
        ),
        cost_estimate=pl.CostEstimate(flops=4 * TOK * D * E, bytes_accessed=3 * 1024 * 1024, transcendentals=0),
    )(step_count, acts, grad_logits, master, moment_one, moment_two)
    count = step_count[0].astype(F32)
    first = 0.9 * moment_one + (1.0 - 0.9) * grad
    second = 0.95 * moment_two + (1.0 - 0.95) * grad * grad
    first_hat = first / (1.0 - jnp.power(0.9, count))
    second_hat = second / (1.0 - jnp.power(0.95, count))
    updated = master - 0.01 * (first_hat / (jnp.sqrt(second_hat) + 1e-08) + 0.1 * master)
    return updated, first, second, logits


def solution(mesh):
    in_specs = (
        P(("seq", "rep"), None),
        P(("seq", "rep"), None),
        P("seq", None),
        P("seq", None),
        P("seq", None),
        P(),
    )
    out_specs = (P("seq", None), P("seq", None), P("seq", None), P(("seq", "rep"), None))
    return jax.shard_map(
        per_device, mesh=mesh, in_specs=in_specs, out_specs=out_specs, check_vma=False
    )
```

```python
import math

import jax
import jax.numpy as jnp
from jax import lax
from jax.experimental import pallas as pl
from jax.experimental.pallas import tpu as pltpu
from jax.sharding import PartitionSpec as P

D = 6144
E = 128
TOK = 256
OWN = 24
UNIT = 48
LEVELS = 32767.0
ROWS = 4 * UNIT
BLK = 384
F32 = jnp.float32
BF16 = jnp.bfloat16
PARTNERS = ((0, 2, 0), (0, 1, 0), (0, 3, 0), (1, 2, 0), (1, 1, 0), (1, 3, 0), (1, 2, 1), (1, 0, 1))
STEPS = (2, 1, 3, 0)
CHUNKS = ((1, 0), (0, 1), (1, 1), (0, 0))
GATHER = ((1, 0), (0, 1), (1, 1), (0, 0))
ORDER = (0, 1, 2, 3, 4, 5, 6, 7, 15, 14, 13, 8, 12, 9, 10, 11)
STEPS = (2, 1, 3, 0)
CHUNKS = ((1, 0), (0, 1), (1, 1), (0, 0))
GATHER = ((1, 0), (0, 1), (1, 1), (0, 0))
ORDER = (0, 1, 2, 3, 4, 5, 6, 7, 15, 14, 13, 8, 12, 9, 10, 11)
NEAR = ((0, 1), (1, 0), (3, 0), (1, 1), (3, 1), (2, 0), (2, 1))


def corrections(count):
    ones = jnp.ones((1, E), F32)
    return 1.0 - jnp.exp(count * math.log(0.9) * ones), 1.0 - jnp.exp(count * math.log(0.95) * ones)


def encode(total):
    most = jnp.max(jnp.abs(total), axis=0, keepdims=True)
    power = jnp.ceil(jnp.log2(jnp.maximum(most, 1e-30)))
    scaled = jnp.clip(total * (LEVELS * jnp.exp2(-power)), -LEVELS, LEVELS)
    codes = jnp.floor(scaled + 0.5).astype(jnp.int32).astype(jnp.int16)
    return codes, jnp.broadcast_to(power.astype(jnp.int32), (16, E)).astype(jnp.int16)


def decode_unit(powers):
    return jnp.exp2(powers.astype(jnp.int32).astype(F32)[:1]) * (1.0 / LEVELS)


def adam(grad, master, one, two, correction_one, correction_two):
    first = 0.9 * one + (1.0 - 0.9) * grad
    second = 0.95 * two + (1.0 - 0.95) * grad * grad
    first_hat = first / correction_one
    second_hat = second / correction_two
    updated = master - 0.01 * (first_hat / (jnp.sqrt(second_hat) + 1e-08) + 0.1 * master)
    return updated, first, second


def kernel(
    step_hbm, acts_hbm, glog_hbm, master_hbm, one_hbm, two_hbm,
    grad_out, logits_out,
    step_ref, acts, glog_ref, part, pair, code, recv_a, acc, recv_b, unit, recv_c, own48, state, state48, grad_own, wnew,
    load_sem, st_sem, ready, s0, r0, sa, ra, sb, rb, sc, rc, sd, rd, sz, rz, s1, r1, s2, r2, s3, r3,
):
    seq = lax.axis_index("seq")
    rep = lax.axis_index("rep")
    core = lax.rem(seq, 2)
    y = rep * 2 + lax.rem(seq // 2, 2)
    z = lax.rem(seq // 4, 16)
    x = seq // 64
    main = (x, y)
    cross = (y, x)

    def dev(px, py, pz, pc):
        return {"seq": ((px * 16 + pz) * 2 + lax.rem(py, 2)) * 2 + pc, "rep": py // 2}

    def at(h, dmain, dcross, dcore):
        dx, dy = (dmain, dcross) if h == 0 else (dcross, dmain)
        return dev(lax.rem(x + dx, 4), lax.rem(y + dy, 4), z, lax.rem(core + dcore, 2))

    def along_z(dz):
        return dev(x, y, lax.rem(z + dz, 16), core)

    def load(src, dst, number):
        copy = pltpu.make_async_copy(src, dst, load_sem.at[number])
        copy.start()
        return copy

    barrier = pltpu.get_barrier_semaphore()
    for h, d, e in PARTNERS:
        pl.semaphore_signal(barrier, inc=1, device_id=at(h, d, 0, e), device_id_type=pl.DeviceIdType.MESH)
    glog_load = load(glog_hbm, glog_ref, 0)
    for k in range(4):
        cols = pl.ds(k * 1536, 1536)
        load(acts_hbm.at[:, cols], acts.at[:, cols], 1)
    for k, ref in enumerate((master_hbm, one_hbm, two_hbm)):
        load(ref, state.at[k], 2)
    step_load = load(step_hbm, step_ref, 3)
    mod = rep * 2 + core
    primary = lax.rem(z, 4) == mod
    rank = sum(jnp.where(z == place, k, 0) for k, place in enumerate(ORDER))
    expected = len(PARTNERS)
    for k, place in enumerate(ORDER):
        meets = jnp.logical_and(z != place, jnp.logical_or(primary, mod == place % 4))

        @pl.when(jnp.logical_and(meets, rank < k))
        def _():
            pl.semaphore_signal(
                barrier, inc=1, device_id=dev(x, y, place, core), device_id_type=pl.DeviceIdType.MESH
            )
        expected = expected + jnp.where(jnp.logical_and(meets, rank > k), 1, 0)

    glog_load.wait()
    glog = glog_ref[...].T

    def remote(src, dst, send, recv, device):
        return pltpu.make_async_remote_copy(
            src_ref=src, dst_ref=dst, send_sem=send, recv_sem=recv,
            device_id=device, device_id_type=pl.DeviceIdType.MESH,
        )

    def arrived(ref, sem):
        remote(ref, ref, sem, sem, along_z(1)).wait_recv()

    def left(ref, sem):
        remote(ref, ref, sem, sem, along_z(1)).wait_send()

    pltpu.make_async_copy(acts_hbm, acts, load_sem.at[1]).wait()
    for h, k in CHUNKS:
        q = h * 2 + k
        for px in range(4):
            cols = pl.ds(px * 1536 + q * BLK, BLK)
            product = jnp.dot(glog, acts[:, cols], preferred_element_type=F32).T.astype(BF16)
            for zr in range(4):
                for ylo in range(2):
                    lo = (zr * 2 + ylo) * UNIT
                    py, pc = (zr // 2) * 2 + ylo, zr % 2
                    which, inner = (px, py) if h == 0 else (py, px)
                    part[q, which * 2 + pc, inner * UNIT:(inner + 1) * UNIT] = product[lo:lo + UNIT]

    pl.semaphore_wait(barrier, expected)
    for h, k in CHUNKS:
        q = h * 2 + k
        for d in STEPS:
            lane = lax.rem(main[h] + d, 4)
            copy = remote(
                part.at[q, lane * 2 + 1 - core], pair.at[q, d], s0.at[0], r0.at[q], at(h, 0, 0, 1)
            )
            copy.start()
    for h, k in CHUNKS:
        q = h * 2 + k
        arrived(pair.at[q], r0.at[q])
        for d in (2, 1, 3):
            total = part[q, lax.rem(main[h] + d, 4) * 2 + core].astype(F32) + pair[q, d].astype(F32)
            code[q, d, :ROWS], code[q, d, ROWS:] = encode(total)
        for d in (2, 1, 3):
            copy = remote(code.at[q, d], recv_a.at[q, d], sa.at[0], ra.at[q], at(h, d, 0, 0))
            copy.start()
    for k, place in enumerate(ORDER):
        @pl.when(jnp.logical_and(primary, rank > k))
        def _():
            pl.semaphore_signal(
                ready.at[z // 4], inc=1, device_id=dev(x, y, place, core), device_id_type=pl.DeviceIdType.MESH
            )

    step_load.wait()
    pltpu.make_async_copy(state, state, load_sem.at[2]).wait()
    half = pl.ds(pl.multiple_of(core * OWN, 8), OWN)
    state48[:, half, :] = state[...]
    state_copy = remote(state, state48.at[:, half, :], st_sem.at[0], st_sem.at[1], at(0, 0, 0, 1))
    state_copy.start()

    for h, k in CHUNKS:
        q = h * 2 + k
        mine = main[h] * 2 + core
        arrived(recv_a.at[q, 1:4], ra.at[q])
        units = {d: decode_unit(recv_a[q, d, ROWS:]) for d in (1, 3, 2)}
        for d in (2, 1, 3, 0):
            to = lax.rem(cross[h] + d, 4)
            rows = pl.ds(pl.multiple_of(to * UNIT, 16), UNIT)
            total = part[q, mine, rows].astype(F32) + pair[q, 0, rows].astype(F32)
            for p in (1, 3, 2):
                total = total + recv_a[q, p, rows].astype(jnp.int32).astype(F32) * units[p]
            acc[q, d] = total
        for d in (2, 1, 3, 0):
            if d:
                copy = remote(acc.at[q, d], recv_b.at[q, d], sb.at[0], rb.at[q], at(h, 0, d, 0))
                copy.start()

    copy_c = []
    for h, k in CHUNKS:
        zg = h * 2 + k
        arrived(recv_b.at[zg, 1:4], rb.at[zg])
        total = ((acc[zg, 0] + recv_b[zg, 1]) + recv_b[zg, 3]) + recv_b[zg, 2]
        unit[zg, :UNIT], unit[zg, UNIT:] = encode(total)
        to = zg * 4 + mod
        dz = lax.rem(to + 16 - z, 16)
        copy = remote(unit.at[zg], recv_c.at[z], sc.at[zg], rc.at[0], dev(x, y, to, core))
        copy_c.append((copy, dz))
        rank_to = sum(jnp.where(to == place, j, 0) for j, place in enumerate(ORDER))

        @pl.when(rank < rank_to)
        def _():
            pl.semaphore_wait(ready.at[zg], 1)

        @pl.when(dz != 0)
        def _():
            copy.start()

        @pl.when(dz == 0)
        def _():
            own48[...] = total

    scales = corrections(step_ref[0].astype(F32))
    state_copy.wait_recv()
    state_copy.wait_send()
    left(pair, s0.at[0])
    left(code.at[0:3], sa.at[0])
    left(acc.at[0:3], sb.at[0])
    other = pl.ds(pl.multiple_of((1 - core) * OWN, 8), OWN)

    def place(zg):
        first = zg // 2 == 0
        which = jnp.where(first, x, y)
        inner = jnp.where(first, y, x)
        return wnew.at[zg, which * 2 + core, pl.ds(pl.multiple_of(inner * UNIT, 16), UNIT)]

    zg_me = z // 4
    spot = place(zg_me)
    copy_z = {
        to: remote(spot, spot, sz.at[0], rz.at[zg_me], dev(x, y, to, core)) for to in range(16)
    }
    copy_d = [
        remote(own48.at[half], grad_own, sd.at[0], rd.at[0], at(1, 2, 0, 0)),
        remote(own48.at[other], grad_own, sd.at[0], rd.at[0], at(1, 0, 0, 1)),
        remote(own48.at[other], grad_own, sd.at[0], rd.at[0], at(1, 2, 0, 1)),
    ]

    @pl.when(primary)
    def _():
        recv_c[z] = jnp.zeros((UNIT + 16, E), jnp.int16)
        arrived(recv_c.at[0:15], rc.at[0])
        total = own48[...]
        for place in range(16):
            total = total + recv_c[place, :UNIT].astype(jnp.int32).astype(F32) * decode_unit(recv_c[place, UNIT:])
        updated, _, _ = adam(total, state48[0], state48[1], state48[2], *scales)
        spot[...] = updated.astype(BF16)
        for to in (0, 1, 2, 3, 4, 15, 5, 14, 6, 13, 7, 12, 8, 11, 9, 10):
            @pl.when(z != to)
            def _():
                copy_z[to].start()
        own48[...] = total
        for copy in copy_d:
            copy.start()
        grad_own[...] = own48[half]

    for h, k in GATHER:
        zg = h * 2 + k

        @pl.when(z != zg * 4 + mod)
        def _():
            remote(place(zg), place(zg), sz.at[0], rz.at[zg], along_z(1)).wait_recv()
        for d in (2, 1, 3):
            copy = remote(place(zg), place(zg), s1.at[0], r1.at[zg], at(h, 0, d, 0))
            copy.start()

    for copy, dz in copy_c:
        @pl.when(dz != 0)
        def _():
            copy.wait_send()

    copy_2 = {}

    def forward(h, k, d):
        q = h * 2 + k
        lane = wnew.at[q, lax.rem(main[h] + d, 4) * 2 + core]
        copy = remote(lane, lane, s3.at[0], r3.at[q], at(h, 0, 0, 1))
        copy.start()

    for h, k in GATHER:
        q = h * 2 + k
        arrived(wnew.at[q, 0, 0:3 * UNIT], r1.at[q])
        mine = wnew.at[q, main[h] * 2 + core]
        for d in (2, 1, 3):
            copy = remote(mine, mine, s2.at[0], r2.at[q, d - 1], at(h, d, 0, 0))
            copy.start()
            copy_2[h, k, d] = copy
        forward(h, k, 0)

    @pl.when(jnp.logical_not(primary))
    def _():
        remote(grad_own, grad_own, sd.at[0], rd.at[0], at(1, 2, 0, 0)).wait_recv()

    grad_out[...] = grad_own[...]

    @pl.when(primary)
    def _():
        left(acts.at[0:240, 0:BLK], sz.at[0])
        left(state, sd.at[0])

    logits = jnp.zeros((TOK, E), F32)

    def apply(total, h, k):
        q = h * 2 + k
        arrived(wnew.at[q, 0:4], r3.at[q])
        for lane in range(4):
            weights = []
            for zr in range(4):
                for ylo in range(2):
                    py, pc = (zr // 2) * 2 + ylo, zr % 2
                    which, inner = (lane, py) if h == 0 else (py, lane)
                    weights.append(wnew[q, which * 2 + pc, inner * UNIT:(inner + 1) * UNIT])
            cols = pl.ds(lane * 1536 + q * BLK, BLK)
            total = total + jnp.dot(acts[:, cols], jnp.concatenate(weights, axis=0), preferred_element_type=F32)
        return total

    for number, (h, k) in enumerate(GATHER):
        for d in (1, 3, 2):
            copy_2[h, k, d].wait_recv()
            forward(h, k, 4 - d)
        if number:
            logits = apply(logits, *GATHER[number - 1])
    logits = apply(logits, *GATHER[-1])
    logits_out[...] = logits.astype(BF16)

    left(wnew.at[0, 0:3], s1.at[0])
    left(wnew.at[0:3, 0:4], s2.at[0])
    left(wnew.at[0:2], s3.at[0])


def per_device(acts, grad_logits, master, moment_one, moment_two, step_count):
    vmem = pl.BlockSpec(memory_space=pltpu.VMEM)
    anywhere = pl.BlockSpec(memory_space=pl.ANY)
    dma = pltpu.SemaphoreType.DMA
    own = jax.ShapeDtypeStruct((OWN, E), F32)
    grad, logits = pl.pallas_call(
        kernel,
        out_shape=(pltpu.VMEM((OWN, E), F32), pltpu.VMEM((TOK, E), BF16)),
        in_specs=[
            anywhere, anywhere, anywhere, anywhere, anywhere, anywhere,
        ],
        out_specs=(vmem, vmem),
        scratch_shapes=[
            pltpu.SMEM((1,), jnp.int32),
            pltpu.VMEM((TOK, D), BF16),
            pltpu.VMEM((TOK, E), BF16),
            pltpu.VMEM((4, 8, ROWS, E), BF16),
            pltpu.VMEM((4, 4, ROWS, E), BF16),
            pltpu.VMEM((4, 4, ROWS + 16, E), jnp.int16),
            pltpu.VMEM((4, 4, ROWS + 16, E), jnp.int16),
            pltpu.VMEM((4, 4, UNIT, E), F32),
            pltpu.VMEM((4, 4, UNIT, E), F32),
            pltpu.VMEM((4, UNIT + 16, E), jnp.int16),
            pltpu.VMEM((16, UNIT + 16, E), jnp.int16),
            pltpu.VMEM((UNIT, E), F32),
            pltpu.VMEM((3, OWN, E), F32),
            pltpu.VMEM((3, UNIT, E), F32),
            pltpu.VMEM((OWN, E), F32),
            pltpu.VMEM((4, 8, 4 * UNIT, E), BF16),
            dma((4,)), dma((2,)), pltpu.SemaphoreType.REGULAR((4,)),
            dma((1,)), dma((4,)),
            dma((1,)), dma((4,)),
            dma((1,)), dma((4,)),
            dma((4,)), dma((1,)),
            dma((1,)), dma((1,)),
            dma((1,)), dma((4,)),
            dma((1,)), dma((4,)),
            dma((1,)), dma((4, 3)),
            dma((1,)), dma((4,)),
        ],
        compiler_params=pltpu.CompilerParams(
            collective_id=0, has_side_effects=True, vmem_limit_bytes=60 * 1024 * 1024
        ),
        cost_estimate=pl.CostEstimate(flops=4 * TOK * D * E, bytes_accessed=3 * 1024 * 1024, transcendentals=0),
    )(step_count, acts, grad_logits, master, moment_one, moment_two)
    count = step_count[0].astype(F32)
    first = 0.9 * moment_one + (1.0 - 0.9) * grad
    second = 0.95 * moment_two + (1.0 - 0.95) * grad * grad
    first_hat = first / (1.0 - jnp.power(0.9, count))
    second_hat = second / (1.0 - jnp.power(0.95, count))
    updated = master - 0.01 * (first_hat / (jnp.sqrt(second_hat) + 1e-08) + 0.1 * master)
    return updated, first, second, logits


def solution(mesh):
    in_specs = (
        P(("seq", "rep"), None),
        P(("seq", "rep"), None),
        P("seq", None),
        P("seq", None),
        P("seq", None),
        P(),
    )
    out_specs = (P("seq", None), P("seq", None), P("seq", None), P(("seq", "rep"), None))
    return jax.shard_map(
        per_device, mesh=mesh, in_specs=in_specs, out_specs=out_specs, check_vma=False
    )
```

```python
import math

import jax
import jax.numpy as jnp
from jax import lax
from jax.experimental import pallas as pl
from jax.experimental.pallas import tpu as pltpu
from jax.sharding import PartitionSpec as P

D = 6144
E = 128
TOK = 256
OWN = 24
UNIT = 48
LEVELS = 32767.0
ROWS = 4 * UNIT
BLK = 384
F32 = jnp.float32
BF16 = jnp.bfloat16
PARTNERS = ((0, 2, 0), (0, 1, 0), (0, 3, 0), (1, 2, 0), (1, 1, 0), (1, 3, 0), (1, 2, 1), (1, 0, 1))
STEPS = (2, 1, 3, 0)
CHUNKS = ((1, 0), (0, 1), (1, 1), (0, 0))
GATHER = ((1, 0), (0, 1), (1, 1), (0, 0))
ORDER = (0, 1, 2, 3, 4, 5, 6, 7, 15, 14, 13, 8, 12, 9, 10, 11)
STEPS = (2, 1, 3, 0)
CHUNKS = ((1, 0), (0, 1), (1, 1), (0, 0))
GATHER = ((1, 0), (0, 1), (1, 1), (0, 0))
ORDER = (0, 1, 2, 3, 4, 5, 6, 7, 15, 14, 13, 8, 12, 9, 10, 11)
NEAR = ((0, 1), (1, 0), (3, 0), (1, 1), (3, 1), (2, 0), (2, 1))


def corrections(count):
    ones = jnp.ones((1, E), F32)
    return 1.0 - jnp.exp(count * math.log(0.9) * ones), 1.0 - jnp.exp(count * math.log(0.95) * ones)


def encode(total):
    most = jnp.max(jnp.abs(total), axis=0, keepdims=True)
    power = jnp.ceil(jnp.log2(jnp.maximum(most, 1e-30)))
    scaled = jnp.clip(total * (LEVELS * jnp.exp2(-power)), -LEVELS, LEVELS)
    codes = jnp.floor(scaled + 0.5).astype(jnp.int32).astype(jnp.int16)
    return codes, jnp.broadcast_to(power.astype(jnp.int32), (16, E)).astype(jnp.int16)


def decode_unit(powers):
    return jnp.exp2(powers.astype(jnp.int32).astype(F32)[:1]) * (1.0 / LEVELS)


def adam(grad, master, one, two, correction_one, correction_two):
    first = 0.9 * one + (1.0 - 0.9) * grad
    second = 0.95 * two + (1.0 - 0.95) * grad * grad
    first_hat = first / correction_one
    second_hat = second / correction_two
    updated = master - 0.01 * (first_hat / (jnp.sqrt(second_hat) + 1e-08) + 0.1 * master)
    return updated, first, second


def kernel(
    step_hbm, acts_hbm, glog_hbm, master_hbm, one_hbm, two_hbm,
    grad_out, logits_out,
    step_ref, acts, glog_ref, part, pair, code, recv_a, acc, held, recv_b, unit, recv_c, own48, state, state48, grad_own, wnew,
    load_sem, st_sem, ready, s0, r0, sa, ra, sb, rb, sc, rc, sd, rd, sz, rz, s1, r1, s2, r2, s3, r3,
):
    seq = lax.axis_index("seq")
    rep = lax.axis_index("rep")
    core = lax.rem(seq, 2)
    y = rep * 2 + lax.rem(seq // 2, 2)
    z = lax.rem(seq // 4, 16)
    x = seq // 64
    main = (x, y)
    cross = (y, x)

    def dev(px, py, pz, pc):
        return {"seq": ((px * 16 + pz) * 2 + lax.rem(py, 2)) * 2 + pc, "rep": py // 2}

    def at(h, dmain, dcross, dcore):
        dx, dy = (dmain, dcross) if h == 0 else (dcross, dmain)
        return dev(lax.rem(x + dx, 4), lax.rem(y + dy, 4), z, lax.rem(core + dcore, 2))

    def along_z(dz):
        return dev(x, y, lax.rem(z + dz, 16), core)

    def load(src, dst, number):
        copy = pltpu.make_async_copy(src, dst, load_sem.at[number])
        copy.start()
        return copy

    barrier = pltpu.get_barrier_semaphore()
    for h, d, e in PARTNERS:
        pl.semaphore_signal(barrier, inc=1, device_id=at(h, d, 0, e), device_id_type=pl.DeviceIdType.MESH)
    glog_load = load(glog_hbm, glog_ref, 0)
    for k in range(4):
        cols = pl.ds(k * 1536, 1536)
        load(acts_hbm.at[:, cols], acts.at[:, cols], 1)
    for k, ref in enumerate((master_hbm, one_hbm, two_hbm)):
        load(ref, state.at[k], 2)
    step_load = load(step_hbm, step_ref, 3)
    mod = rep * 2 + core
    primary = lax.rem(z, 4) == mod
    rank = sum(jnp.where(z == place, k, 0) for k, place in enumerate(ORDER))
    expected = len(PARTNERS)
    for k, place in enumerate(ORDER):
        meets = jnp.logical_and(z != place, jnp.logical_or(primary, mod == place % 4))

        @pl.when(jnp.logical_and(meets, rank < k))
        def _():
            pl.semaphore_signal(
                barrier, inc=1, device_id=dev(x, y, place, core), device_id_type=pl.DeviceIdType.MESH
            )
        expected = expected + jnp.where(jnp.logical_and(meets, rank > k), 1, 0)

    glog_load.wait()
    glog = glog_ref[...].T

    def remote(src, dst, send, recv, device):
        return pltpu.make_async_remote_copy(
            src_ref=src, dst_ref=dst, send_sem=send, recv_sem=recv,
            device_id=device, device_id_type=pl.DeviceIdType.MESH,
        )

    def arrived(ref, sem):
        remote(ref, ref, sem, sem, along_z(1)).wait_recv()

    def left(ref, sem):
        remote(ref, ref, sem, sem, along_z(1)).wait_send()

    pltpu.make_async_copy(acts_hbm, acts, load_sem.at[1]).wait()
    for h, k in CHUNKS:
        q = h * 2 + k
        for px in range(4):
            cols = pl.ds(px * 1536 + q * BLK, BLK)
            product = jnp.dot(glog, acts[:, cols], preferred_element_type=F32).T.astype(BF16)
            for zr in range(4):
                for ylo in range(2):
                    lo = (zr * 2 + ylo) * UNIT
                    py, pc = (zr // 2) * 2 + ylo, zr % 2
                    which, inner = (px, py) if h == 0 else (py, px)
                    part[q, which * 2 + pc, inner * UNIT:(inner + 1) * UNIT] = product[lo:lo + UNIT]

    pl.semaphore_wait(barrier, expected)
    for h, k in CHUNKS:
        q = h * 2 + k
        for d in STEPS:
            lane = lax.rem(main[h] + d, 4)
            copy = remote(
                part.at[q, lane * 2 + 1 - core], pair.at[q, d], s0.at[0], r0.at[q], at(h, 0, 0, 1)
            )
            copy.start()
    for h, k in CHUNKS:
        q = h * 2 + k
        arrived(pair.at[q], r0.at[q])
        for d in (2, 1, 3):
            total = part[q, lax.rem(main[h] + d, 4) * 2 + core].astype(F32) + pair[q, d].astype(F32)
            code[q, d, :ROWS], code[q, d, ROWS:] = encode(total)
        for d in (2, 1, 3):
            copy = remote(code.at[q, d], recv_a.at[q, d], sa.at[0], ra.at[q], at(h, d, 0, 0))
            copy.start()
    for k, place in enumerate(ORDER):
        @pl.when(jnp.logical_and(primary, rank > k))
        def _():
            pl.semaphore_signal(
                ready.at[z // 4], inc=1, device_id=dev(x, y, place, core), device_id_type=pl.DeviceIdType.MESH
            )

    step_load.wait()
    pltpu.make_async_copy(state, state, load_sem.at[2]).wait()
    half = pl.ds(pl.multiple_of(core * OWN, 8), OWN)
    state48[:, half, :] = state[...]
    state_copy = remote(state, state48.at[:, half, :], st_sem.at[0], st_sem.at[1], at(0, 0, 0, 1))
    state_copy.start()

    for h, k in CHUNKS:
        q = h * 2 + k
        mine = main[h] * 2 + core
        arrived(recv_a.at[q, 1:4], ra.at[q])
        units = {d: decode_unit(recv_a[q, d, ROWS:]) for d in (1, 3, 2)}
        for d in (2, 1, 3, 0):
            to = lax.rem(cross[h] + d, 4)
            rows = pl.ds(pl.multiple_of(to * UNIT, 16), UNIT)
            total = part[q, mine, rows].astype(F32) + pair[q, 0, rows].astype(F32)
            for p in (1, 3, 2):
                total = total + recv_a[q, p, rows].astype(jnp.int32).astype(F32) * units[p]
            if d:
                acc[q, d - 1, :UNIT], acc[q, d - 1, UNIT:] = encode(total)
            else:
                held[q] = total
        for d in (2, 1, 3, 0):
            if d:
                copy = remote(acc.at[q, d - 1], recv_b.at[q, d - 1], sb.at[0], rb.at[q], at(h, 0, d, 0))
                copy.start()

    copy_c = []
    for h, k in CHUNKS:
        zg = h * 2 + k
        arrived(recv_b.at[zg], rb.at[zg])
        total = held[zg]
        for d in range(3):
            total = total + recv_b[zg, d, :UNIT].astype(jnp.int32).astype(F32) * decode_unit(recv_b[zg, d, UNIT:])
        unit[zg, :UNIT], unit[zg, UNIT:] = encode(total)
        to = zg * 4 + mod
        dz = lax.rem(to + 16 - z, 16)
        copy = remote(unit.at[zg], recv_c.at[z], sc.at[zg], rc.at[0], dev(x, y, to, core))
        copy_c.append((copy, dz))
        rank_to = sum(jnp.where(to == place, j, 0) for j, place in enumerate(ORDER))

        @pl.when(rank < rank_to)
        def _():
            pl.semaphore_wait(ready.at[zg], 1)

        @pl.when(dz != 0)
        def _():
            copy.start()

        @pl.when(dz == 0)
        def _():
            own48[...] = total

    scales = corrections(step_ref[0].astype(F32))
    state_copy.wait_recv()
    state_copy.wait_send()
    left(pair, s0.at[0])
    left(code.at[0:3], sa.at[0])
    left(acc, sb.at[0])
    other = pl.ds(pl.multiple_of((1 - core) * OWN, 8), OWN)

    def place(zg):
        first = zg // 2 == 0
        which = jnp.where(first, x, y)
        inner = jnp.where(first, y, x)
        return wnew.at[zg, which * 2 + core, pl.ds(pl.multiple_of(inner * UNIT, 16), UNIT)]

    zg_me = z // 4
    spot = place(zg_me)
    copy_z = {
        to: remote(spot, spot, sz.at[0], rz.at[zg_me], dev(x, y, to, core)) for to in range(16)
    }
    copy_d = [
        remote(own48.at[half], grad_own, sd.at[0], rd.at[0], at(1, 2, 0, 0)),
        remote(own48.at[other], grad_own, sd.at[0], rd.at[0], at(1, 0, 0, 1)),
        remote(own48.at[other], grad_own, sd.at[0], rd.at[0], at(1, 2, 0, 1)),
    ]

    @pl.when(primary)
    def _():
        recv_c[z] = jnp.zeros((UNIT + 16, E), jnp.int16)
        arrived(recv_c.at[0:15], rc.at[0])
        total = own48[...]
        for place in range(16):
            total = total + recv_c[place, :UNIT].astype(jnp.int32).astype(F32) * decode_unit(recv_c[place, UNIT:])
        updated, _, _ = adam(total, state48[0], state48[1], state48[2], *scales)
        spot[...] = updated.astype(BF16)
        for to in (0, 1, 2, 3, 4, 15, 5, 14, 6, 13, 7, 12, 8, 11, 9, 10):
            @pl.when(z != to)
            def _():
                copy_z[to].start()
        own48[...] = total
        for copy in copy_d:
            copy.start()
        grad_own[...] = own48[half]

    for h, k in GATHER:
        zg = h * 2 + k

        @pl.when(z != zg * 4 + mod)
        def _():
            remote(place(zg), place(zg), sz.at[0], rz.at[zg], along_z(1)).wait_recv()
        for d in (2, 1, 3):
            copy = remote(place(zg), place(zg), s1.at[0], r1.at[zg], at(h, 0, d, 0))
            copy.start()

    for copy, dz in copy_c:
        @pl.when(dz != 0)
        def _():
            copy.wait_send()

    copy_2 = {}

    def forward(h, k, d):
        q = h * 2 + k
        lane = wnew.at[q, lax.rem(main[h] + d, 4) * 2 + core]
        copy = remote(lane, lane, s3.at[0], r3.at[q], at(h, 0, 0, 1))
        copy.start()

    for h, k in GATHER:
        q = h * 2 + k
        arrived(wnew.at[q, 0, 0:3 * UNIT], r1.at[q])
        mine = wnew.at[q, main[h] * 2 + core]
        for d in (2, 1, 3):
            copy = remote(mine, mine, s2.at[0], r2.at[q, d - 1], at(h, d, 0, 0))
            copy.start()
            copy_2[h, k, d] = copy
        forward(h, k, 0)

    @pl.when(jnp.logical_not(primary))
    def _():
        remote(grad_own, grad_own, sd.at[0], rd.at[0], at(1, 2, 0, 0)).wait_recv()

    grad_out[...] = grad_own[...]

    @pl.when(primary)
    def _():
        left(acts.at[0:240, 0:BLK], sz.at[0])
        left(state, sd.at[0])

    logits = jnp.zeros((TOK, E), F32)

    def apply(total, h, k):
        q = h * 2 + k
        arrived(wnew.at[q, 0:4], r3.at[q])
        for lane in range(4):
            weights = []
            for zr in range(4):
                for ylo in range(2):
                    py, pc = (zr // 2) * 2 + ylo, zr % 2
                    which, inner = (lane, py) if h == 0 else (py, lane)
                    weights.append(wnew[q, which * 2 + pc, inner * UNIT:(inner + 1) * UNIT])
            cols = pl.ds(lane * 1536 + q * BLK, BLK)
            total = total + jnp.dot(acts[:, cols], jnp.concatenate(weights, axis=0), preferred_element_type=F32)
        return total

    for number, (h, k) in enumerate(GATHER):
        for d in (1, 3, 2):
            copy_2[h, k, d].wait_recv()
            forward(h, k, 4 - d)
        if number:
            logits = apply(logits, *GATHER[number - 1])
    logits = apply(logits, *GATHER[-1])
    logits_out[...] = logits.astype(BF16)

    left(wnew.at[0, 0:3], s1.at[0])
    left(wnew.at[0:3, 0:4], s2.at[0])
    left(wnew.at[0:2], s3.at[0])


def per_device(acts, grad_logits, master, moment_one, moment_two, step_count):
    vmem = pl.BlockSpec(memory_space=pltpu.VMEM)
    anywhere = pl.BlockSpec(memory_space=pl.ANY)
    dma = pltpu.SemaphoreType.DMA
    own = jax.ShapeDtypeStruct((OWN, E), F32)
    grad, logits = pl.pallas_call(
        kernel,
        out_shape=(pltpu.VMEM((OWN, E), F32), pltpu.VMEM((TOK, E), BF16)),
        in_specs=[
            anywhere, anywhere, anywhere, anywhere, anywhere, anywhere,
        ],
        out_specs=(vmem, vmem),
        scratch_shapes=[
            pltpu.SMEM((1,), jnp.int32),
            pltpu.VMEM((TOK, D), BF16),
            pltpu.VMEM((TOK, E), BF16),
            pltpu.VMEM((4, 8, ROWS, E), BF16),
            pltpu.VMEM((4, 4, ROWS, E), BF16),
            pltpu.VMEM((4, 4, ROWS + 16, E), jnp.int16),
            pltpu.VMEM((4, 4, ROWS + 16, E), jnp.int16),
            pltpu.VMEM((4, 3, UNIT + 16, E), jnp.int16),
            pltpu.VMEM((4, UNIT, E), F32),
            pltpu.VMEM((4, 3, UNIT + 16, E), jnp.int16),
            pltpu.VMEM((4, UNIT + 16, E), jnp.int16),
            pltpu.VMEM((16, UNIT + 16, E), jnp.int16),
            pltpu.VMEM((UNIT, E), F32),
            pltpu.VMEM((3, OWN, E), F32),
            pltpu.VMEM((3, UNIT, E), F32),
            pltpu.VMEM((OWN, E), F32),
            pltpu.VMEM((4, 8, 4 * UNIT, E), BF16),
            dma((4,)), dma((2,)), pltpu.SemaphoreType.REGULAR((4,)),
            dma((1,)), dma((4,)),
            dma((1,)), dma((4,)),
            dma((1,)), dma((4,)),
            dma((4,)), dma((1,)),
            dma((1,)), dma((1,)),
            dma((1,)), dma((4,)),
            dma((1,)), dma((4,)),
            dma((1,)), dma((4, 3)),
            dma((1,)), dma((4,)),
        ],
        compiler_params=pltpu.CompilerParams(
            collective_id=0, has_side_effects=True, vmem_limit_bytes=60 * 1024 * 1024
        ),
        cost_estimate=pl.CostEstimate(flops=4 * TOK * D * E, bytes_accessed=3 * 1024 * 1024, transcendentals=0),
    )(step_count, acts, grad_logits, master, moment_one, moment_two)
    count = step_count[0].astype(F32)
    first = 0.9 * moment_one + (1.0 - 0.9) * grad
    second = 0.95 * moment_two + (1.0 - 0.95) * grad * grad
    first_hat = first / (1.0 - jnp.power(0.9, count))
    second_hat = second / (1.0 - jnp.power(0.95, count))
    updated = master - 0.01 * (first_hat / (jnp.sqrt(second_hat) + 1e-08) + 0.1 * master)
    return updated, first, second, logits


def solution(mesh):
    in_specs = (
        P(("seq", "rep"), None),
        P(("seq", "rep"), None),
        P("seq", None),
        P("seq", None),
        P("seq", None),
        P(),
    )
    out_specs = (P("seq", None), P("seq", None), P("seq", None), P(("seq", "rep"), None))
    return jax.shard_map(
        per_device, mesh=mesh, in_specs=in_specs, out_specs=out_specs, check_vma=False
    )
```
